32 devices in a mesh: segment: 2 (over x), tm: 4 (over z), space: 4 (over y, core).
Axes of the slice: x: 2, y: 2, z: 4, core: 2. Of those that a mesh axis runs over, the one named last changes fastest.
Arguments:
- clip_frames: bfloat16 [16, 32, 128, 128], P('tm', 'space'), may hold values from -6 to 6
- enc_weight: bfloat16 [3, 3, 3, 128, 256], replicated, may hold values from -0.109375 to 0.109375
- dec_weight: bfloat16 [3, 3, 3, 256, 128], replicated, may hold values from -0.078125 to 0.078125
- out_grad: bfloat16 [8, 16, 64, 128], P('tm', 'space'), may hold values from -6 to 6
Outputs:
- latent_pair: bfloat16 [2, 8, 16, 64, 256], P('segment', 'tm', 'space')
- weight_grads: float32 [2, 27, 32768], P('segment')
The draws below stay inside these ranges and needn't reach their ends.
All inputs are finite; a program needn't handle non-finite values.
Results may differ from the reference program's by a relative error of at most 0.0056.
Values may be sent and summed in bfloat16 or wider, within the bound.
A program may use at most 128 MiB of HBM per device.

```python
import math
import jax
import jax.numpy as jnp
from jax import lax

C_IN = 128
C_LAT = 256
WL = 64
TL = 8
HL = 16
T_IN = 16
H_IN = 32
W_IN = 128


def block_scale(own_key, dims, cuts, smallest, largest):
    def one(position, shards_of):
        draws = jax.random.uniform(jax.random.fold_in(jax.random.fold_in(own_key, 6), position), (shards_of,), jnp.float32, smallest / len(cuts), largest / len(cuts))
        return jnp.repeat(jnp.exp(draws), dims[position] // shards_of).reshape((-1,) + (1,) * (len(dims) - position - 1))

    factor_of = one(*cuts[0])
    for cut in cuts[1:]:
        factor_of = factor_of * one(*cut)
    return factor_of


def bell_draw(own_key, shape, spread, bound, cuts=(), held_as=jnp.bfloat16):
    entries = jax.random.normal(own_key, shape, jnp.float32) * spread
    if len(cuts) > 0:
        entries = block_scale(own_key, shape, cuts, -0.22, 0.18) * entries
    return jnp.clip(entries, min=-bound, max=bound).astype(held_as)


def setup_inputs(seed: int = 0) -> dict:
    arg_keys = jax.random.split(jax.random.key(seed), 5)
    return {
        "clip_frames": bell_draw(arg_keys[0], (T_IN, H_IN, W_IN, C_IN), 1.0, 6.0, ((0, 4), (1, 4))),
        "enc_weight": bell_draw(arg_keys[1], (3, 3, 3, C_IN, C_LAT), (27 * C_IN) ** -0.5, 0.109375),
        "dec_weight": bell_draw(arg_keys[2], (3, 3, 3, C_LAT, C_IN), (27 * C_LAT) ** -0.5, 0.078125),
        "out_grad": bell_draw(arg_keys[3], (TL, HL, WL, C_IN), 1.0, 6.0, ((0, 4), (1, 4))),
    }


def encode_taps(padded, enc_weight, frame_count, row_count, col_count):
    chans = padded.shape[-1]
    summed = jnp.zeros((frame_count * row_count * col_count, enc_weight.shape[-1]), jnp.float32)
    for tap_t in range(3):
        for tap_h in range(3):
            for tap_w in range(3):
                window = padded[tap_t:tap_t + 2 * frame_count:2, tap_h:tap_h + 2 * row_count:2, tap_w:tap_w + 2 * col_count:2]
                summed = summed + jnp.dot(window.reshape(-1, chans), enc_weight[tap_t, tap_h, tap_w], preferred_element_type=jnp.float32)
    return summed.reshape(frame_count, row_count, col_count, -1).astype(jnp.bfloat16)

def decode_taps(extended, dec_weight, out_grad):
    frame_count, row_count, col_count, out_chans = out_grad.shape
    chans = extended.shape[-1]
    pre_act = jnp.zeros((frame_count * row_count * col_count, out_chans), jnp.float32)
    for tap_t in range(3):
        for tap_h in range(3):
            for tap_w in range(3):
                window = extended[tap_t:tap_t + frame_count, tap_h:tap_h + row_count, tap_w:tap_w + col_count]
                pre_act = pre_act + jnp.dot(window.reshape(-1, chans), dec_weight[tap_t, tap_h, tap_w], preferred_element_type=jnp.float32)
    sigm = jax.nn.sigmoid(pre_act)
    slope = out_grad.reshape(-1, out_chans).astype(jnp.float32) * sigm * (1.0 + pre_act * (1.0 - sigm))
    return slope.astype(jnp.bfloat16).reshape(out_grad.shape)

def transpose_taps(rimmed, dec_weight, frame_count, row_count, col_count):
    chans = rimmed.shape[-1]
    summed = jnp.zeros((frame_count * row_count * col_count, dec_weight.shape[3]), jnp.float32)
    for tap_t in range(3):
        for tap_h in range(3):
            for tap_w in range(3):
                window = rimmed[2 - tap_t:2 - tap_t + frame_count, 2 - tap_h:2 - tap_h + row_count, 2 - tap_w:2 - tap_w + col_count]
                summed = summed + lax.dot_general(window.reshape(-1, chans), dec_weight[tap_t, tap_h, tap_w], (((1,), (1,)), ((), ())), preferred_element_type=jnp.float32)
    return summed.reshape(frame_count, row_count, col_count, -1).astype(jnp.bfloat16)

def enc_taps_grad(padded, lat_grad):
    frame_count, row_count, col_count, lat_chans = lat_grad.shape
    chans = padded.shape[-1]
    flat_grad = lat_grad.reshape(-1, lat_chans)
    pieces = []
    for tap_t in range(3):
        for tap_h in range(3):
            for tap_w in range(3):
                window = padded[tap_t:tap_t + 2 * frame_count:2, tap_h:tap_h + 2 * row_count:2, tap_w:tap_w + 2 * col_count:2]
                pieces.append(lax.dot_general(window.reshape(-1, chans), flat_grad, (((0,), (0,)), ((), ())), preferred_element_type=jnp.float32).reshape(-1))
    return jnp.stack(pieces)

def dec_taps_grad(extended, slope):
    frame_count, row_count, col_count, out_chans = slope.shape
    chans = extended.shape[-1]
    flat_slope = slope.reshape(-1, out_chans)
    pieces = []
    for tap_t in range(3):
        for tap_h in range(3):
            for tap_w in range(3):
                window = extended[tap_t:tap_t + frame_count, tap_h:tap_h + row_count, tap_w:tap_w + col_count]
                pieces.append(lax.dot_general(window.reshape(-1, chans), flat_slope, (((0,), (0,)), ((), ())), preferred_element_type=jnp.float32).reshape(-1))
    return jnp.stack(pieces)

def reference(clip_frames, enc_weight, dec_weight, out_grad):
    padded = jnp.pad(clip_frames, ((2, 0), (1, 1), (1, 1), (0, 0)))
    latent = encode_taps(padded, enc_weight, TL, HL, WL)
    extended = jnp.pad(latent, ((2, 0), (1, 1), (1, 1), (0, 0)))
    slope = decode_taps(extended, dec_weight, out_grad)
    rimmed = jnp.pad(slope, ((0, 2), (1, 1), (1, 1), (0, 0)))
    lat_grad = transpose_taps(rimmed, dec_weight, TL, HL, WL)
    enc_grad = enc_taps_grad(padded, lat_grad)
    dec_grad = dec_taps_grad(extended, slope)
    grad_scale = 1.0 / math.sqrt(TL * HL * WL)
    weight_grads = jnp.stack([enc_grad, dec_grad]) * grad_scale
    latent_pair = jnp.stack([lat_grad, latent])
    return (latent_pair, weight_grads)
```

```python
import functools
import math

import jax
import jax.numpy as jnp
from jax import lax
from jax.experimental import pallas as pl
from jax.experimental.pallas import tpu as pltpu
from jax.sharding import PartitionSpec as P

MESH = pl.DeviceIdType.MESH
BF = jnp.bfloat16
F32 = jnp.float32
TAPS = 27
ROWS = TAPS * 256


def mm(x, y):
    return jnp.dot(x, y, preferred_element_type=F32)


def kernel(
    T,
    S,
    sh,
    scale,
    clip,
    ew_h,
    dw_h,
    og_h,
    latp,
    wout,
    clipx,
    x3,
    ew,
    dw,
    og,
    pout,
    pin,
    ext,
    rim,
    s3,
    lg,
    gt,
    st,
    part,
    rcv1,
    red,
    rcv2,
    gat,
    out4,
    lsem,
    ssem,
    rsem,
    c_ss,
    c_rs,
    a_ss,
    a_rs,
    g_ss,
    g_rs,
    osem,
):
    seg = lax.axis_index("segment")
    k = lax.axis_index("tm")
    s = lax.axis_index("space")
    n = T * S
    Q = n // 2
    half = Q * sh
    core = s % 2
    q = k * (S // 2) + s // 2
    has_up, has_dn = s > 0, s < S - 1
    has_pv, has_nx = k > 0, k < T - 1
    is_enc = seg == 0

    loads = [
        pltpu.make_async_copy(clip, clipx.at[:, pl.ds(1, 8)], lsem.at[0]),
        pltpu.make_async_copy(ew_h, ew, lsem.at[1]),
        pltpu.make_async_copy(dw_h, dw, lsem.at[2]),
        pltpu.make_async_copy(og_h, og, lsem.at[3]),
    ]
    for c in loads:
        c.start()

    me = k * S + s
    barrier = pltpu.get_barrier_semaphore()

    def greet(d, carry):
        peer = (me + d) % n
        pl.semaphore_signal(
            barrier, inc=1, device_id=(seg, peer // S, peer % S), device_id_type=MESH
        )
        return carry

    lax.fori_loop(1, n, greet, 0)
    pl.semaphore_wait(barrier, n - 1)

    def remote(src, dst, i, to):
        return pltpu.make_async_remote_copy(
            src_ref=src,
            dst_ref=dst,
            send_sem=ssem.at[i],
            recv_sem=rsem.at[i],
            device_id=to,
            device_id_type=MESH,
        )

    def launch(entries):
        for copy, sends, gets, dst in entries:

            @pl.when(sends)
            def _():
                copy.start()

    def collect(entries):
        for copy, sends, gets, dst in entries:

            @pl.when(gets)
            def _():
                copy.wait_recv()

            @pl.when(jnp.logical_not(gets))
            def _():
                dst[...] = jnp.zeros(dst.shape, dst.dtype)

    def drain(entries):
        for copy, sends, gets, dst in entries:

            @pl.when(sends)
            def _():
                copy.wait_send()

    def entry(src, there, i, to, sends, gets):
        return (remote(src, there, i, to), sends, gets, there)

    e_clip = [
        entry(clip.at[:, pl.ds(7, 1)], clipx.at[:, pl.ds(0, 1)], 0, (seg, k, s + 1), has_dn, has_up)
    ]
    launch(e_clip)

    sel_i = lax.broadcasted_iota(jnp.int32, (192, 128), 0)
    sel_j = lax.broadcasted_iota(jnp.int32, (192, 128), 1)
    sel = (sel_j == 2 * (sel_i % 64) + sel_i // 64 - 1).astype(F32).astype(BF)

    def split_cols(f, r):
        y = mm(sel, clipx[f, r]).astype(BF)
        x3[f, r] = jnp.concatenate([y[:64], y[64:128], y[128:]], axis=1)

    loads[0].wait()

    def split_frame(f, carry):
        for r in range(1, 9):
            split_cols(f, r)
        return carry

    lax.fori_loop(0, 4, split_frame, 0)
    collect(e_clip)
    for f in range(4):
        split_cols(f, 0)
    loads[1].wait()

    def xrows(f, b):
        return jnp.concatenate([x3[f, b + 2 * h] for h in range(4)], axis=0)

    acc = jnp.zeros((256, 256), F32)
    for a in range(2):
        for b in range(3):
            acc = acc + mm(xrows(2 + a, b), ew[3 * a + b])
    pout[...] = acc
    e_part = [entry(pout, pin, 1, (seg, k + 1, s), has_nx, has_pv)]
    launch(e_part)

    def lat_entries(f, base):
        own = 2 + f
        return [
            entry(ext.at[own, pl.ds(1, 4)], ext.at[f, pl.ds(1, 4)], base, (seg, k + 1, s), has_nx, has_pv),
            entry(ext.at[own, pl.ds(4, 1)], ext.at[own, pl.ds(0, 1)], base + 1, (seg, k, s + 1), has_dn, has_up),
            entry(ext.at[own, pl.ds(1, 1)], ext.at[own, pl.ds(5, 1)], base + 2, (seg, k, s - 1), has_up, has_dn),
            entry(
                ext.at[own, pl.ds(4, 1)],
                ext.at[f, pl.ds(0, 1)],
                base + 3,
                (seg, k + 1, s + 1),
                has_nx & has_dn,
                has_pv & has_up,
            ),
            entry(
                ext.at[own, pl.ds(1, 1)],
                ext.at[f, pl.ds(5, 1)],
                base + 4,
                (seg, k + 1, s - 1),
                has_nx & has_up,
                has_pv & has_dn,
            ),
        ]

    acc = jnp.zeros((256, 256), F32)
    for a in range(3):
        for b in range(3):
            acc = acc + mm(xrows(a, b), ew[3 * a + b])
    ext[3, 1:5] = acc.astype(BF).reshape(4, 64, 256)
    e_lat1 = lat_entries(1, 2)
    launch(e_lat1)

    acc = jnp.zeros((256, 256), F32)
    for b in range(3):
        acc = acc + mm(xrows(0, b), ew[6 + b])
    collect(e_part)
    ext[2, 1:5] = (acc + pin[...]).astype(BF).reshape(4, 64, 256)
    e_lat0 = lat_entries(0, 7)
    launch(e_lat0)

    loads[2].wait()
    loads[3].wait()
    collect(e_lat1)
    collect(e_lat0)

    col = lax.broadcasted_iota(jnp.int32, (256, 128), 0) % 64

    def dcat(ab):
        return jnp.concatenate([dw[3 * ab], dw[3 * ab + 1], dw[3 * ab + 2]], axis=1)

    def erows(f, b):
        return jnp.concatenate([ext[f, b + h] for h in range(4)], axis=0)

    for t in range(2):
        acc = jnp.zeros((256, 384), F32)
        for a in range(3):
            for b in range(3):
                acc = acc + mm(erows(t + a, b), dcat(3 * a + b))
        before = jnp.where(col == 0, 0.0, pltpu.roll(acc[:, :128], 1, 0))
        after = jnp.where(col == 63, 0.0, pltpu.roll(acc[:, 256:], 255, 0))
        pre = before + acc[:, 128:256] + after
        sg = jax.nn.sigmoid(pre)
        slope = og[t].reshape(256, 128).astype(F32) * sg * (1.0 + pre * (1.0 - sg))
        rim[t, 1:5] = slope.astype(BF).reshape(4, 64, 128)

    col64 = lax.broadcasted_iota(jnp.int32, (64, 128), 0)

    def shifts(v):
        later = jnp.where(col64 == 63, 0.0, pltpu.roll(v, 63, 0))
        sooner = jnp.where(col64 == 0, 0.0, pltpu.roll(v, 1, 0))
        return jnp.concatenate([later, v, sooner], axis=1)

    e_slope = [
        entry(rim.at[pl.ds(0, 2), pl.ds(1, 4)], rim.at[pl.ds(2, 2), pl.ds(1, 4)], 12, (seg, k - 1, s), has_pv, has_nx),
        entry(rim.at[pl.ds(0, 2), pl.ds(4, 1)], rim.at[pl.ds(0, 2), pl.ds(0, 1)], 13, (seg, k, s + 1), has_dn, has_up),
        entry(rim.at[pl.ds(0, 2), pl.ds(1, 1)], rim.at[pl.ds(0, 2), pl.ds(5, 1)], 14, (seg, k, s - 1), has_up, has_dn),
        entry(
            rim.at[pl.ds(0, 2), pl.ds(4, 1)],
            rim.at[pl.ds(2, 2), pl.ds(0, 1)],
            15,
            (seg, k - 1, s + 1),
            has_pv & has_dn,
            has_nx & has_up,
        ),
        entry(
            rim.at[pl.ds(0, 2), pl.ds(1, 1)],
            rim.at[pl.ds(2, 2), pl.ds(5, 1)],
            16,
            (seg, k - 1, s - 1),
            has_pv & has_up,
            has_nx & has_dn,
        ),
    ]
    e_lg = [entry(lg.at[0], lg.at[2], 17, (seg, k - 1, s), has_pv, has_nx)]

    @pl.when(is_enc)
    def _():
        launch(e_slope)
        for f in range(2):
            for r in range(1, 5):
                s3[f, r] = shifts(rim[f, r].astype(F32)).astype(BF)
        collect(e_slope)
        for f in range(2):
            for r in (0, 5):
                s3[f, r] = shifts(rim[f, r].astype(F32)).astype(BF)
        for f in range(2, 4):
            for r in range(6):
                s3[f, r] = shifts(rim[f, r].astype(F32)).astype(BF)
        for t in range(2):
            acc = jnp.zeros((256, 256), F32)
            for a in range(3):
                for b in range(3):
                    rows = jnp.concatenate([s3[t + 2 - a, h + 2 - b] for h in range(4)], axis=0)
                    acc = acc + lax.dot_general(
                        rows, dcat(3 * a + b), (((1,), (1,)), ((), ())), preferred_element_type=F32
                    )
            rounded = acc.astype(BF)
            lg[t] = rounded.reshape(4, 64, 256)
            if t == 0:
                launch(e_lg)
            gt[:, t * 256 : (t + 1) * 256] = rounded.astype(F32).T.astype(BF)
        out_lat = pltpu.make_async_copy(lg.at[pl.ds(0, 2)], latp, osem.at[0])
        out_lat.start()

        def enc_block(a, b, frames, lanes):
            cells = jnp.concatenate([xrows(f, b) for f in frames], axis=0)
            grad = mm(gt[:, lanes * 256 : lanes * 256 + 512], cells)
            for c in range(3):
                whole = grad[:, c * 128 : (c + 1) * 128].T.astype(BF)
                at = (3 * (3 * a + b) + c) * 256
                part[at : at + 128, :] = whole[:, :128]
                part[at + 128 : at + 256, :] = whole[:, 128:]

        for b in range(3):
            enc_block(2, b, (0, 2), 0)
        collect(e_lg)
        gt[:, 512:768] = lg[2].reshape(256, 256).astype(F32).T.astype(BF)
        for b in range(3):
            enc_block(0, b, (0, 2), 1)
        for b in range(3):
            enc_block(1, b, (1, 3), 1)
        drain(e_slope)
        drain(e_lg)
        out_lat.wait()

    @pl.when(jnp.logical_not(is_enc))
    def _():
        out_lat = pltpu.make_async_copy(ext.at[pl.ds(2, 2), pl.ds(1, 4)], latp, osem.at[0])
        out_lat.start()
        for t in range(2):
            cells = jnp.concatenate([shifts(rim[t, 1 + h].astype(F32)) for h in range(4)], axis=0)
            st[:, t * 256 : (t + 1) * 256] = cells.T.astype(BF)
        for a in range(3):
            for b in range(3):
                cells = jnp.concatenate([erows(a, b), erows(1 + a, b)], axis=0)
                grad = mm(st[...], cells)
                for c in range(3):
                    at = (3 * (3 * a + b) + c) * 256
                    part[at : at + 256, :] = grad[c * 128 : (c + 1) * 128].T.astype(BF)
        out_lat.wait()

    drain(e_clip)
    drain(e_part)
    drain(e_lat1)
    drain(e_lat0)

    if n * sh > ROWS:
        part[ROWS:, :] = jnp.zeros((n * sh - ROWS, 128), BF)

    def al(x):
        return pl.multiple_of(x, 16)

    sibling = (seg, k, s + 1 - 2 * core)
    swap = pltpu.make_async_remote_copy(
        src_ref=part.at[pl.ds(al((1 - core) * half), half)],
        dst_ref=rcv1,
        send_sem=c_ss.at[0],
        recv_sem=c_rs.at[0],
        device_id=sibling,
        device_id_type=MESH,
    )
    swap.start()
    swap.wait()
    red[...] = (part[pl.ds(al(core * half), half), :].astype(F32) + rcv1[...].astype(F32)).astype(BF)

    def chip(p):
        return (seg, p // (S // 2), 2 * (p % (S // 2)) + core)

    scatter = []
    for d in range(1, Q):
        p = (q + d) % Q
        scatter.append(
            pltpu.make_async_remote_copy(
                src_ref=red.at[pl.ds(al(p * sh), sh)],
                dst_ref=rcv2.at[d - 1],
                send_sem=a_ss.at[d - 1],
                recv_sem=a_rs.at[d - 1],
                device_id=chip(p),
                device_id_type=MESH,
            )
        )
    for copy in scatter:
        copy.start()
    total = red[pl.ds(al(q * sh), sh), :].astype(F32)
    for d in range(1, Q):
        scatter[d - 1].wait_recv()
        total = total + rcv2[d - 1].astype(F32)
    mine = pl.ds(al((core * Q + q) * sh), sh)
    gat[mine, :] = (total * scale).astype(BF)

    spread = []
    for d in range(1, Q):
        p = (q + d) % Q
        spread.append(
            pltpu.make_async_remote_copy(
                src_ref=gat.at[mine],
                dst_ref=gat.at[mine],
                send_sem=g_ss.at[d - 1],
                recv_sem=g_rs.at[d - 1],
                device_id=chip(p),
                device_id_type=MESH,
            )
        )
    for copy in spread:
        copy.start()
    for d in range(1, Q):
        theirs = gat.at[pl.ds(al((core * Q + (q - d + Q) % Q) * sh), sh)]
        pltpu.make_async_remote_copy(
            src_ref=theirs,
            dst_ref=theirs,
            send_sem=g_ss.at[d - 1],
            recv_sem=g_rs.at[d - 1],
            device_id=sibling,
            device_id_type=MESH,
        ).wait_recv()
    own_half = gat.at[pl.ds(al(core * half), half)]
    other_half = gat.at[pl.ds(al((1 - core) * half), half)]
    give = pltpu.make_async_remote_copy(
        src_ref=own_half,
        dst_ref=own_half,
        send_sem=c_ss.at[1],
        recv_sem=c_rs.at[1],
        device_id=sibling,
        device_id_type=MESH,
    )
    give.start()
    pltpu.make_async_remote_copy(
        src_ref=other_half,
        dst_ref=other_half,
        send_sem=c_ss.at[1],
        recv_sem=c_rs.at[1],
        device_id=sibling,
        device_id_type=MESH,
    ).wait_recv()

    out4[3] = jnp.zeros((2048, 128), F32)

    @pl.when(is_enc)
    def _():
        for i in range(TAPS):
            for hh in range(2):
                v = gat[i * 256 + hh * 128 : i * 256 + hh * 128 + 128, :].astype(F32)
                out4[i // 8, pl.ds(hh * 8 + i % 8, 128, stride=16), :] = v

    @pl.when(jnp.logical_not(is_enc))
    def _():
        for i in range(TAPS):
            v = gat[i * 256 : i * 256 + 256, :].astype(F32)
            out4[i // 8, pl.ds(i % 8, 256, stride=8), :] = v

    out_w = pltpu.make_async_copy(out4, wout, osem.at[1])
    out_w.start()
    for copy in scatter:
        copy.wait_send()
    for copy in spread:
        copy.wait_send()
    give.wait_send()
    out_w.wait()


def solution(mesh):
    T, S = mesh.shape["tm"], mesh.shape["space"]
    n = T * S
    sh = -(-ROWS // n // 16) * 16
    Q = n // 2

    def on_device(clip_frames, enc_weight, dec_weight, out_grad):
        scale = 1.0 / math.sqrt(2 * 4 * 64 * n)
        dma = pltpu.SemaphoreType.DMA
        latp, wout = pl.pallas_call(
            functools.partial(kernel, T, S, sh, scale),
            out_shape=(
                jax.ShapeDtypeStruct((2, 4, 64, 256), BF),
                jax.ShapeDtypeStruct((4, 2048, 128), F32),
            ),
            in_specs=[pl.BlockSpec(memory_space=pl.ANY)] * 4,
            out_specs=(pl.BlockSpec(memory_space=pl.ANY),) * 2,
            scratch_shapes=[
                pltpu.VMEM((4, 9, 128, 128), BF),
                pltpu.VMEM((4, 9, 64, 384), BF),
                pltpu.VMEM((9, 384, 256), BF),
                pltpu.VMEM((27, 256, 128), BF),
                pltpu.VMEM((2, 4, 64, 128), BF),
                pltpu.VMEM((256, 256), F32),
                pltpu.VMEM((256, 256), F32),
                pltpu.VMEM((4, 6, 64, 256), BF),
                pltpu.VMEM((4, 6, 64, 128), BF),
                pltpu.VMEM((4, 6, 64, 384), BF),
                pltpu.VMEM((3, 4, 64, 256), BF),
                pltpu.VMEM((256, 768), BF),
                pltpu.VMEM((384, 512), BF),
                pltpu.VMEM((n * sh, 128), BF),
                pltpu.VMEM((Q * sh, 128), BF),
                pltpu.VMEM((Q * sh, 128), BF),
                pltpu.VMEM((Q - 1, sh, 128), BF),
                pltpu.VMEM((n * sh, 128), BF),
                pltpu.VMEM((4, 2048, 128), F32),
                dma((4,)),
                dma((18,)),
                dma((18,)),
                dma((2,)),
                dma((2,)),
                dma((Q - 1,)),
                dma((Q - 1,)),
                dma((Q - 1,)),
                dma((Q - 1,)),
                dma((2,)),
            ],
            compiler_params=pltpu.CompilerParams(
                collective_id=0, has_side_effects=True, vmem_limit_bytes=48 * 1024 * 1024
            ),
            cost_estimate=pl.CostEstimate(
                flops=5 * 10**9, bytes_accessed=12 * 10**6, transcendentals=65536
            ),
        )(
            clip_frames,
            enc_weight.reshape(9, 384, 256),
            dec_weight.reshape(27, 256, 128),
            out_grad,
        )
        flat = wout.reshape(4, 256, 8, 128).transpose(0, 2, 1, 3).reshape(32, 32768)
        return latp[None], flat[None, :TAPS]

    placed = (P("tm", "space", None, None), P(), P(), P("tm", "space", None, None))
    return jax.shard_map(
        on_device,
        mesh=mesh,
        in_specs=placed,
        out_specs=(P("segment", "tm", "space", None, None), P("segment", None, None)),
        check_vma=False,
    )
```

```python
import functools
import math

import jax
import jax.numpy as jnp
from jax import lax
from jax.experimental import pallas as pl
from jax.experimental.pallas import tpu as pltpu
from jax.sharding import PartitionSpec as P

MESH = pl.DeviceIdType.MESH
BF = jnp.bfloat16
F32 = jnp.float32
TAPS = 27
CHUNK = 9 * 256


def mm(x, y):
    return jnp.dot(x, y, preferred_element_type=F32)


def kernel(
    T,
    S,
    sh,
    scale,
    clip,
    ew_h,
    dw_h,
    og_h,
    latp,
    wout,
    clipx,
    x3,
    ew,
    dw,
    og,
    pout,
    pin,
    ext,
    rim,
    s3,
    lg,
    gt,
    st,
    mix,
    part,
    rcv1,
    red1,
    rcvy,
    red2,
    rcvz,
    gat,
    lsem,
    ssem,
    rsem,
    c_sem,
    y_sem,
    z_sem,
    gz_sem,
    gy_sem,
    gc_sem,
    osem,
):
    seg = lax.axis_index("segment")
    k = lax.axis_index("tm")
    s = lax.axis_index("space")
    n = T * S
    Y = S // 2
    half = n // 2 * sh
    core = s % 2
    y = s // 2
    has_up, has_dn = s > 0, s < S - 1
    has_pv, has_nx = k > 0, k < T - 1
    is_enc = seg == 0

    loads = [
        pltpu.make_async_copy(clip, clipx.at[:, pl.ds(1, 8)], lsem.at[0]),
        pltpu.make_async_copy(ew_h, ew, lsem.at[1]),
        pltpu.make_async_copy(dw_h, dw, lsem.at[2]),
        pltpu.make_async_copy(og_h, og, lsem.at[3]),
    ]
    for c in loads:
        c.start()

    me = k * S + s
    barrier = pltpu.get_barrier_semaphore()

    def greet(d, carry):
        peer = (me + d) % n
        pl.semaphore_signal(
            barrier, inc=1, device_id=(seg, peer // S, peer % S), device_id_type=MESH
        )
        return carry

    lax.fori_loop(1, n, greet, 0)
    pl.semaphore_wait(barrier, n - 1)

    def remote(src, dst, i, to):
        return pltpu.make_async_remote_copy(
            src_ref=src,
            dst_ref=dst,
            send_sem=ssem.at[i],
            recv_sem=rsem.at[i],
            device_id=to,
            device_id_type=MESH,
        )

    def launch(entries):
        for copy, sends, gets, dst in entries:

            @pl.when(sends)
            def _():
                copy.start()

    def collect(entries):
        for copy, sends, gets, dst in entries:

            @pl.when(gets)
            def _():
                copy.wait_recv()

            @pl.when(jnp.logical_not(gets))
            def _():
                dst[...] = jnp.zeros(dst.shape, dst.dtype)

    def drain(entries):
        for copy, sends, gets, dst in entries:

            @pl.when(sends)
            def _():
                copy.wait_send()

    def entry(src, there, i, to, sends, gets):
        return (remote(src, there, i, to), sends, gets, there)

    e_clip = [
        entry(clip.at[:, pl.ds(7, 1)], clipx.at[:, pl.ds(0, 1)], 0, (seg, k, s + 1), has_dn, has_up)
    ]
    launch(e_clip)

    sel_i = lax.broadcasted_iota(jnp.int32, (192, 128), 0)
    sel_j = lax.broadcasted_iota(jnp.int32, (192, 128), 1)
    sel = (sel_j == 2 * (sel_i % 64) + sel_i // 64 - 1).astype(F32).astype(BF)

    def split_cols(f, r):
        y = mm(sel, clipx[f, r]).astype(BF)
        x3[f, r] = jnp.concatenate([y[:64], y[64:128], y[128:]], axis=1)

    loads[0].wait()

    def split_frame(f, carry):
        for r in range(1, 9):
            split_cols(f, r)
        return carry

    lax.fori_loop(0, 4, split_frame, 0)
    collect(e_clip)
    for f in range(4):
        split_cols(f, 0)
    loads[1].wait()

    def xrows(f, b):
        return jnp.concatenate([x3[f, b + 2 * h] for h in range(4)], axis=0)

    acc = jnp.zeros((256, 256), F32)
    for a in range(2):
        for b in range(3):
            acc = acc + mm(xrows(2 + a, b), ew[3 * a + b])
    pout[...] = acc.astype(BF)
    e_part = [entry(pout, pin, 1, (seg, k + 1, s), has_nx, has_pv)]
    launch(e_part)

    def lat_entries(f, base):
        own = 2 + f
        return [
            entry(ext.at[own, pl.ds(1, 4)], ext.at[f, pl.ds(1, 4)], base, (seg, k + 1, s), has_nx, has_pv),
            entry(ext.at[own, pl.ds(4, 1)], ext.at[own, pl.ds(0, 1)], base + 1, (seg, k, s + 1), has_dn, has_up),
            entry(ext.at[own, pl.ds(1, 1)], ext.at[own, pl.ds(5, 1)], base + 2, (seg, k, s - 1), has_up, has_dn),
            entry(
                ext.at[own, pl.ds(4, 1)],
                ext.at[f, pl.ds(0, 1)],
                base + 3,
                (seg, k + 1, s + 1),
                has_nx & has_dn,
                has_pv & has_up,
            ),
            entry(
                ext.at[own, pl.ds(1, 1)],
                ext.at[f, pl.ds(5, 1)],
                base + 4,
                (seg, k + 1, s - 1),
                has_nx & has_up,
                has_pv & has_dn,
            ),
        ]

    acc = jnp.zeros((256, 256), F32)
    for a in range(3):
        for b in range(3):
            acc = acc + mm(xrows(a, b), ew[3 * a + b])
    ext[3, 1:5] = acc.astype(BF).reshape(4, 64, 256)
    e_lat1 = lat_entries(1, 2)
    launch(e_lat1)

    acc = jnp.zeros((256, 256), F32)
    for b in range(3):
        acc = acc + mm(xrows(0, b), ew[6 + b])
    collect(e_part)
    ext[2, 1:5] = (acc + pin[...].astype(F32)).astype(BF).reshape(4, 64, 256)
    e_lat0 = lat_entries(0, 7)
    launch(e_lat0)

    loads[2].wait()
    loads[3].wait()
    collect(e_lat1)
    collect(e_lat0)

    col = lax.broadcasted_iota(jnp.int32, (256, 128), 0) % 64

    def dcat(ab):
        return jnp.concatenate([dw[3 * ab], dw[3 * ab + 1], dw[3 * ab + 2]], axis=1)

    def erows(f, b):
        return jnp.concatenate([ext[f, b + h] for h in range(4)], axis=0)

    for t in range(2):
        acc = jnp.zeros((256, 384), F32)
        for a in range(3):
            for b in range(3):
                acc = acc + mm(erows(t + a, b), dcat(3 * a + b))
        before = jnp.where(col == 0, 0.0, pltpu.roll(acc[:, :128], 1, 0))
        after = jnp.where(col == 63, 0.0, pltpu.roll(acc[:, 256:], 255, 0))
        pre = before + acc[:, 128:256] + after
        sg = jax.nn.sigmoid(pre)
        slope = og[t].reshape(256, 128).astype(F32) * sg * (1.0 + pre * (1.0 - sg))
        rim[t, 1:5] = slope.astype(BF).reshape(4, 64, 128)

    col64 = lax.broadcasted_iota(jnp.int32, (64, 128), 0)

    def shifts(v):
        later = jnp.where(col64 == 63, 0.0, pltpu.roll(v, 63, 0))
        sooner = jnp.where(col64 == 0, 0.0, pltpu.roll(v, 1, 0))
        return jnp.concatenate([later, v, sooner], axis=1)

    e_slope = [
        entry(rim.at[pl.ds(0, 2), pl.ds(1, 4)], rim.at[pl.ds(2, 2), pl.ds(1, 4)], 12, (seg, k - 1, s), has_pv, has_nx),
        entry(rim.at[pl.ds(0, 2), pl.ds(4, 1)], rim.at[pl.ds(0, 2), pl.ds(0, 1)], 13, (seg, k, s + 1), has_dn, has_up),
        entry(rim.at[pl.ds(0, 2), pl.ds(1, 1)], rim.at[pl.ds(0, 2), pl.ds(5, 1)], 14, (seg, k, s - 1), has_up, has_dn),
        entry(
            rim.at[pl.ds(0, 2), pl.ds(4, 1)],
            rim.at[pl.ds(2, 2), pl.ds(0, 1)],
            15,
            (seg, k - 1, s + 1),
            has_pv & has_dn,
            has_nx & has_up,
        ),
        entry(
            rim.at[pl.ds(0, 2), pl.ds(1, 1)],
            rim.at[pl.ds(2, 2), pl.ds(5, 1)],
            16,
            (seg, k - 1, s - 1),
            has_pv & has_up,
            has_nx & has_dn,
        ),
    ]
    e_lg = [entry(lg.at[0], lg.at[2], 17, (seg, k - 1, s), has_pv, has_nx)]

    @pl.when(is_enc)
    def _():
        launch(e_slope)
        for f in range(2):
            for r in range(1, 5):
                s3[f, r] = shifts(rim[f, r].astype(F32)).astype(BF)
        collect(e_slope)
        for f in range(2):
            for r in (0, 5):
                s3[f, r] = shifts(rim[f, r].astype(F32)).astype(BF)
        for f in range(2, 4):
            for r in range(6):
                s3[f, r] = shifts(rim[f, r].astype(F32)).astype(BF)
        for t in range(2):
            acc = jnp.zeros((256, 256), F32)
            for a in range(3):
                for b in range(3):
                    rows = jnp.concatenate([s3[t + 2 - a, h + 2 - b] for h in range(4)], axis=0)
                    acc = acc + lax.dot_general(
                        rows, dcat(3 * a + b), (((1,), (1,)), ((), ())), preferred_element_type=F32
                    )
            rounded = acc.astype(BF)
            lg[t] = rounded.reshape(4, 64, 256)
            if t == 0:
                launch(e_lg)
            gt[:, t * 256 : (t + 1) * 256] = rounded.astype(F32).T.astype(BF)
        pltpu.make_async_copy(lg.at[pl.ds(0, 2)], latp, osem.at[0]).start()

    @pl.when(jnp.logical_not(is_enc))
    def _():
        pltpu.make_async_copy(ext.at[pl.ds(2, 2), pl.ds(1, 4)], latp, osem.at[0]).start()
        for t in range(2):
            cells = jnp.concatenate([shifts(rim[t, 1 + h].astype(F32)) for h in range(4)], axis=0)
            st[:, t * 256 : (t + 1) * 256] = cells.T.astype(BF)

    def enc_block(a, b, frames, lanes):
        cells = jnp.concatenate([xrows(f, b) for f in frames], axis=0)
        grad = mm(gt[:, lanes * 256 : lanes * 256 + 512], cells)
        for c in range(3):
            whole = grad[:, c * 128 : (c + 1) * 128].T
            mix[c, pl.ds(0, 128, stride=2), :] = whole[:, :128]
            mix[c, pl.ds(1, 128, stride=2), :] = whole[:, 128:]
            at = (3 * b + c) * 256
            part[a, at : at + 256, :] = mix[c].astype(BF)

    def dec_block(a, b):
        cells = jnp.concatenate([erows(a, b), erows(1 + a, b)], axis=0)
        grad = mm(st[...], cells)
        for c in range(3):
            at = (3 * b + c) * 256
            part[a, at : at + 256, :] = grad[c * 128 : (c + 1) * 128].T.astype(BF)

    def grads(a):
        @pl.when(is_enc)
        def _():
            if a == 0:
                collect(e_lg)
                gt[:, 512:768] = lg[2].reshape(256, 256).astype(F32).T.astype(BF)
            for b in range(3):
                enc_block(a, b, (1, 3) if a == 1 else (0, 2), 0 if a == 2 else 1)

        @pl.when(jnp.logical_not(is_enc))
        def _():
            for b in range(3):
                dec_block(a, b)

        if n * sh > CHUNK:
            part[a, CHUNK:, :] = jnp.zeros((n * sh - CHUNK, 128), BF)

    def rows(start, count):
        return pl.ds(pl.multiple_of(start, 16), count)

    def move(src, dst, sems, i, to):
        return pltpu.make_async_remote_copy(
            src_ref=src,
            dst_ref=dst,
            send_sem=sems.at[0, i],
            recv_sem=sems.at[1, i],
            device_id=to,
            device_id_type=MESH,
        )

    sibling = (seg, k, s + 1 - 2 * core)
    sent = []

    def send(copy):
        copy.start()
        sent.append(copy)

    def arrived(dst, sems, i):
        move(dst, dst, sems, i, sibling).wait_recv()

    def at_y(p):
        return (seg, k, 2 * p + core)

    def core_start(a):
        send(move(part.at[a, rows((1 - core) * half, half)], rcv1.at[a], c_sem, a, sibling))

    def y_start(a):
        arrived(rcv1.at[a], c_sem, a)
        red1[a] = (part[a, rows(core * half, half), :].astype(F32) + rcv1[a].astype(F32)).astype(BF)
        for d in range(1, Y):
            p = (y + d) % Y
            i = a * (Y - 1) + d - 1
            send(move(red1.at[a, rows(p * T * sh, T * sh)], rcvy.at[i], y_sem, i, at_y(p)))

    def z_start(a):
        total = red1[a, rows(y * T * sh, T * sh), :].astype(F32)
        for d in range(1, Y):
            i = a * (Y - 1) + d - 1
            arrived(rcvy.at[i], y_sem, i)
            total = total + rcvy[i].astype(F32)
        red2[a] = total.astype(BF)
        for d in range(1, T):
            p = (k + d) % T
            i = a * (T - 1) + d - 1
            send(move(red2.at[a, rows(p * sh, sh)], rcvz.at[i], z_sem, i, (seg, p, s)))

    def shard(a, py, pz):
        return gat.at[a, rows(((core * Y + py) * T + pz) * sh, sh)]

    def band(a, pc, py):
        return gat.at[a, rows((pc * Y + py) * T * sh, T * sh)]

    def gz_start(a):
        total = red2[a, rows(k * sh, sh), :].astype(F32)
        for d in range(1, T):
            i = a * (T - 1) + d - 1
            arrived(rcvz.at[i], z_sem, i)
            total = total + rcvz[i].astype(F32)
        gat[a, rows(((core * Y + y) * T + k) * sh, sh), :] = (total * scale).astype(BF)
        for d in range(1, T):
            i = a * (T - 1) + d - 1
            send(move(shard(a, y, k), shard(a, y, k), gz_sem, i, (seg, (k + d) % T, s)))

    def gy_start(a):
        for d in range(1, T):
            arrived(shard(a, y, (k - d + T) % T), gz_sem, a * (T - 1) + d - 1)
        for d in range(1, Y):
            send(move(band(a, core, y), band(a, core, y), gy_sem, a * (Y - 1) + d - 1, at_y((y + d) % Y)))
        send(move(band(a, core, y), band(a, core, y), gc_sem, a * Y, sibling))

    def gc_start(a):
        for d in range(1, Y):
            theirs = band(a, core, (y - d + Y) % Y)
            arrived(theirs, gy_sem, a * (Y - 1) + d - 1)
            send(move(theirs, theirs, gc_sem, a * Y + d, sibling))

    def finish(a):
        for d in range(Y):
            arrived(band(a, 1 - core, (y - d + Y) % Y), gc_sem, a * Y + d)
        pltpu.make_async_copy(gat.at[a], wout.at[a], osem.at[1 + a]).start()

    stages = [grads, core_start, y_start, z_start, gz_start, gy_start, gc_start, finish]
    order = (2, 0, 1)
    for step in range(len(stages) + 2):
        if step < 3:
            grads(order[step])
            core_start(order[step])
        for j in range(3):
            stage = step - j
            if 1 <= stage < len(stages) - 1:
                stages[stage + 1](order[j])

    for copy in sent:
        copy.wait_send()

    @pl.when(is_enc)
    def _():
        drain(e_slope)
        drain(e_lg)

    drain(e_clip)
    drain(e_part)
    drain(e_lat1)
    drain(e_lat0)
    pltpu.make_async_copy(lg.at[pl.ds(0, 2)], latp, osem.at[0]).wait()
    for a in range(3):
        pltpu.make_async_copy(gat.at[a], wout.at[a], osem.at[1 + a]).wait()


def solution(mesh):
    T, S = mesh.shape["tm"], mesh.shape["space"]
    n = T * S
    sh = -(-CHUNK // n // 16) * 16
    Y = S // 2
    half = n // 2 * sh

    def on_device(clip_frames, enc_weight, dec_weight, out_grad):
        scale = 1.0 / math.sqrt(2 * 4 * 64 * n)
        dma = pltpu.SemaphoreType.DMA
        latp, wout = pl.pallas_call(
            functools.partial(kernel, T, S, sh, scale),
            out_shape=(
                jax.ShapeDtypeStruct((2, 4, 64, 256), BF),
                jax.ShapeDtypeStruct((3, n * sh, 128), BF),
            ),
            in_specs=[pl.BlockSpec(memory_space=pl.ANY)] * 4,
            out_specs=(pl.BlockSpec(memory_space=pl.ANY),) * 2,
            scratch_shapes=[
                pltpu.VMEM((4, 9, 128, 128), BF),
                pltpu.VMEM((4, 9, 64, 384), BF),
                pltpu.VMEM((9, 384, 256), BF),
                pltpu.VMEM((27, 256, 128), BF),
                pltpu.VMEM((2, 4, 64, 128), BF),
                pltpu.VMEM((256, 256), BF),
                pltpu.VMEM((256, 256), BF),
                pltpu.VMEM((4, 6, 64, 256), BF),
                pltpu.VMEM((4, 6, 64, 128), BF),
                pltpu.VMEM((4, 6, 64, 384), BF),
                pltpu.VMEM((3, 4, 64, 256), BF),
                pltpu.VMEM((256, 768), BF),
                pltpu.VMEM((384, 512), BF),
                pltpu.VMEM((3, 256, 128), F32),
                pltpu.VMEM((3, n * sh, 128), BF),
                pltpu.VMEM((3, half, 128), BF),
                pltpu.VMEM((3, half, 128), BF),
                pltpu.VMEM((3 * (Y - 1), T * sh, 128), BF),
                pltpu.VMEM((3, T * sh, 128), BF),
                pltpu.VMEM((3 * (T - 1), sh, 128), BF),
                pltpu.VMEM((3, n * sh, 128), BF),
                dma((4,)),
                dma((18,)),
                dma((18,)),
                dma((2, 3)),
                dma((2, 3 * (Y - 1))),
                dma((2, 3 * (T - 1))),
                dma((2, 3 * (T - 1))),
                dma((2, 3 * (Y - 1))),
                dma((2, 3 * Y)),
                dma((4,)),
            ],
            compiler_params=pltpu.CompilerParams(
                collective_id=0, has_side_effects=True, vmem_limit_bytes=60 * 1024 * 1024
            ),
            cost_estimate=pl.CostEstimate(
                flops=5 * 10**9, bytes_accessed=12 * 10**6, transcendentals=65536
            ),
        )(
            clip_frames,
            enc_weight.reshape(9, 384, 256),
            dec_weight.reshape(27, 256, 128),
            out_grad,
        )
        flat = wout[:, :CHUNK].reshape(1, TAPS, 32768).astype(F32)
        return latp[None], flat

    placed = (P("tm", "space", None, None), P(), P(), P("tm", "space", None, None))
    return jax.shard_map(
        on_device,
        mesh=mesh,
        in_specs=placed,
        out_specs=(P("segment", "tm", "space", None, None), P("segment", None, None)),
        check_vma=False,
    )
```

```python
import functools
import math

import jax
import jax.numpy as jnp
from jax import lax
from jax.experimental import pallas as pl
from jax.experimental.pallas import tpu as pltpu
from jax.sharding import PartitionSpec as P

MESH = pl.DeviceIdType.MESH
BF = jnp.bfloat16
F32 = jnp.float32
TAPS = 27
BLOCK = 3 * 256
CHUNKS = (
    ((2, 0),),
    ((2, 1), (2, 2)),
    ((0, 0), (0, 1)),
    ((0, 2), (1, 0)),
    ((1, 1),),
    ((1, 2),),
)


def mm(x, y):
    return jnp.dot(x, y, preferred_element_type=F32)


def kernel(
    T,
    S,
    shards,
    scale,
    clip,
    ew_h,
    dw_h,
    og_h,
    latp,
    wout,
    clipx,
    x3,
    ew,
    dw,
    og,
    pout,
    pin,
    ext,
    rim,
    s3,
    lg,
    gt,
    st,
    mix,
    part,
    rcv1,
    red1,
    rcvy,
    red2,
    rcvz,
    gat,
    lsem,
    ssem,
    rsem,
    c_sem,
    y_sem,
    z_sem,
    gz_sem,
    gy_sem,
    gc_sem,
    osem,
):
    seg = lax.axis_index("segment")
    k = lax.axis_index("tm")
    s = lax.axis_index("space")
    n = T * S
    Y = S // 2
    core = s % 2
    y = s // 2
    has_up, has_dn = s > 0, s < S - 1
    has_pv, has_nx = k > 0, k < T - 1
    is_enc = seg == 0

    loads = [
        pltpu.make_async_copy(clip, clipx.at[:, pl.ds(1, 8)], lsem.at[0]),
        pltpu.make_async_copy(ew_h, ew, lsem.at[1]),
        pltpu.make_async_copy(dw_h, dw, lsem.at[2]),
        pltpu.make_async_copy(og_h, og, lsem.at[3]),
    ]
    for c in loads:
        c.start()

    me = k * S + s
    barrier = pltpu.get_barrier_semaphore()

    def greet(d, carry):
        peer = (me + d) % n
        pl.semaphore_signal(
            barrier, inc=1, device_id=(seg, peer // S, peer % S), device_id_type=MESH
        )
        return carry

    lax.fori_loop(1, n, greet, 0)
    pl.semaphore_wait(barrier, n - 1)

    def remote(src, dst, i, to):
        return pltpu.make_async_remote_copy(
            src_ref=src,
            dst_ref=dst,
            send_sem=ssem.at[i],
            recv_sem=rsem.at[i],
            device_id=to,
            device_id_type=MESH,
        )

    def launch(entries):
        for copy, sends, gets, dst in entries:

            @pl.when(sends)
            def _():
                copy.start()

    def collect(entries):
        for copy, sends, gets, dst in entries:

            @pl.when(gets)
            def _():
                copy.wait_recv()

            @pl.when(jnp.logical_not(gets))
            def _():
                dst[...] = jnp.zeros(dst.shape, dst.dtype)

    def drain(entries):
        for copy, sends, gets, dst in entries:

            @pl.when(sends)
            def _():
                copy.wait_send()

    def entry(src, there, i, to, sends, gets):
        return (remote(src, there, i, to), sends, gets, there)

    e_clip = [
        entry(clip.at[:, pl.ds(7, 1)], clipx.at[:, pl.ds(0, 1)], 0, (seg, k, s + 1), has_dn, has_up)
    ]
    launch(e_clip)

    sel_i = lax.broadcasted_iota(jnp.int32, (192, 128), 0)
    sel_j = lax.broadcasted_iota(jnp.int32, (192, 128), 1)
    sel = (sel_j == 2 * (sel_i % 64) + sel_i // 64 - 1).astype(F32).astype(BF)

    def split_cols(f, r):
        y = mm(sel, clipx[f, r]).astype(BF)
        x3[f, r] = jnp.concatenate([y[:64], y[64:128], y[128:]], axis=1)

    loads[0].wait()

    def split_frame(f, carry):
        for r in range(1, 9):
            split_cols(f, r)
        return carry

    lax.fori_loop(0, 4, split_frame, 0)
    collect(e_clip)
    for f in range(4):
        split_cols(f, 0)
    loads[1].wait()

    def xrows(f, b):
        return jnp.concatenate([x3[f, b + 2 * h] for h in range(4)], axis=0)

    acc = jnp.zeros((256, 256), F32)
    for a in range(2):
        for b in range(3):
            acc = acc + mm(xrows(2 + a, b), ew[3 * a + b])
    pout[...] = acc.astype(BF)
    e_part = [entry(pout, pin, 1, (seg, k + 1, s), has_nx, has_pv)]
    launch(e_part)

    def lat_entries(f, base):
        own = 2 + f
        return [
            entry(ext.at[own, pl.ds(1, 4)], ext.at[f, pl.ds(1, 4)], base, (seg, k + 1, s), has_nx, has_pv),
            entry(ext.at[own, pl.ds(4, 1)], ext.at[own, pl.ds(0, 1)], base + 1, (seg, k, s + 1), has_dn, has_up),
            entry(ext.at[own, pl.ds(1, 1)], ext.at[own, pl.ds(5, 1)], base + 2, (seg, k, s - 1), has_up, has_dn),
            entry(
                ext.at[own, pl.ds(4, 1)],
                ext.at[f, pl.ds(0, 1)],
                base + 3,
                (seg, k + 1, s + 1),
                has_nx & has_dn,
                has_pv & has_up,
            ),
            entry(
                ext.at[own, pl.ds(1, 1)],
                ext.at[f, pl.ds(5, 1)],
                base + 4,
                (seg, k + 1, s - 1),
                has_nx & has_up,
                has_pv & has_dn,
            ),
        ]

    acc = jnp.zeros((256, 256), F32)
    for a in range(3):
        for b in range(3):
            acc = acc + mm(xrows(a, b), ew[3 * a + b])
    ext[3, 1:5] = acc.astype(BF).reshape(4, 64, 256)
    e_lat1 = lat_entries(1, 2)
    launch(e_lat1)

    acc = jnp.zeros((256, 256), F32)
    for b in range(3):
        acc = acc + mm(xrows(0, b), ew[6 + b])
    collect(e_part)
    ext[2, 1:5] = (acc + pin[...].astype(F32)).astype(BF).reshape(4, 64, 256)
    e_lat0 = lat_entries(0, 7)
    launch(e_lat0)

    loads[2].wait()
    loads[3].wait()
    col = lax.broadcasted_iota(jnp.int32, (256, 128), 0) % 64

    def dcat(ab):
        return jnp.concatenate([dw[3 * ab], dw[3 * ab + 1], dw[3 * ab + 2]], axis=1)

    def erows(f, b):
        return jnp.concatenate([ext[f, b + h] for h in range(4)], axis=0)

    def decode(acc, t, taps_t):
        for a in taps_t:
            for b in range(3):
                acc = acc + mm(erows(t + a, b), dcat(3 * a + b))
        return acc

    def slope_of(acc, t):
        before = jnp.where(col == 0, 0.0, pltpu.roll(acc[:, :128], 1, 0))
        after = jnp.where(col == 63, 0.0, pltpu.roll(acc[:, 256:], 255, 0))
        pre = before + acc[:, 128:256] + after
        sg = jax.nn.sigmoid(pre)
        slope = og[t].reshape(256, 128).astype(F32) * sg * (1.0 + pre * (1.0 - sg))
        rim[t, 1:5] = slope.astype(BF).reshape(4, 64, 128)

    def slope_entries(f, base):
        own = rim.at[f, pl.ds(1, 4)]
        top = rim.at[f, pl.ds(1, 1)]
        last = rim.at[f, pl.ds(4, 1)]
        far = 2 + f
        return [
            entry(own, rim.at[far, pl.ds(1, 4)], base, (seg, k - 1, s), has_pv, has_nx),
            entry(last, rim.at[f, pl.ds(0, 1)], base + 1, (seg, k, s + 1), has_dn, has_up),
            entry(top, rim.at[f, pl.ds(5, 1)], base + 2, (seg, k, s - 1), has_up, has_dn),
            entry(last, rim.at[far, pl.ds(0, 1)], base + 3, (seg, k - 1, s + 1), has_pv & has_dn, has_nx & has_up),
            entry(top, rim.at[far, pl.ds(5, 1)], base + 4, (seg, k - 1, s - 1), has_pv & has_up, has_nx & has_dn),
        ]

    e_slope1 = slope_entries(1, 12)
    e_slope0 = slope_entries(0, 17)
    e_lg = [entry(lg.at[0], lg.at[2], 22, (seg, k - 1, s), has_pv, has_nx)]

    collect(e_lat1[1:3])
    collect(e_lat0[1:3])
    zero = jnp.zeros((256, 384), F32)
    acc1 = decode(zero, 1, (1, 2))
    acc0 = decode(zero, 0, (2,))
    collect(e_lat1[:1] + e_lat1[3:])
    slope_of(decode(acc1, 1, (0,)), 1)

    @pl.when(is_enc)
    def _():
        launch(e_slope1)

    acc0 = decode(acc0, 0, (1,))
    collect(e_lat0[:1] + e_lat0[3:])
    slope_of(decode(acc0, 0, (0,)), 0)

    @pl.when(is_enc)
    def _():
        launch(e_slope0)

    col64 = lax.broadcasted_iota(jnp.int32, (64, 128), 0)

    def shifts(v):
        later = jnp.where(col64 == 63, 0.0, pltpu.roll(v, 63, 0))
        sooner = jnp.where(col64 == 0, 0.0, pltpu.roll(v, 1, 0))
        return jnp.concatenate([later, v, sooner], axis=1)

    def put_shifts(f, which):
        for r in which:
            s3[f, r] = shifts(rim[f, r].astype(F32)).astype(BF)

    def transpose(acc, t, taps_t):
        for a in taps_t:
            for b in range(3):
                cells = jnp.concatenate([s3[t + 2 - a, h + 2 - b] for h in range(4)], axis=0)
                acc = acc + lax.dot_general(
                    cells, dcat(3 * a + b), (((1,), (1,)), ((), ())), preferred_element_type=F32
                )
        return acc

    def keep(acc, t):
        rounded = acc.astype(BF)
        lg[t] = rounded.reshape(4, 64, 256)
        if t == 0:
            launch(e_lg)
        gt[:, t * 256 : (t + 1) * 256] = rounded.astype(F32).T.astype(BF)

    @pl.when(is_enc)
    def _():
        for f in (1, 0):
            put_shifts(f, range(1, 5))
        collect(e_slope1[1:3])
        collect(e_slope0[1:3])
        for f in (1, 0):
            put_shifts(f, (0, 5))
        zero = jnp.zeros((256, 256), F32)
        acc0 = transpose(zero, 0, (1, 2))
        acc1 = transpose(zero, 1, (2,))
        collect(e_slope1[:1] + e_slope1[3:])
        put_shifts(3, range(6))
        collect(e_slope0[:1] + e_slope0[3:])
        put_shifts(2, range(6))
        keep(transpose(acc0, 0, (0,)), 0)
        keep(transpose(acc1, 1, (0, 1)), 1)
        pltpu.make_async_copy(lg.at[pl.ds(0, 2)], latp, osem.at[0]).start()

    @pl.when(jnp.logical_not(is_enc))
    def _():
        pltpu.make_async_copy(ext.at[pl.ds(2, 2), pl.ds(1, 4)], latp, osem.at[0]).start()
        for t in range(2):
            cells = jnp.concatenate([shifts(rim[t, 1 + h].astype(F32)) for h in range(4)], axis=0)
            st[:, t * 256 : (t + 1) * 256] = cells.T.astype(BF)

    def enc_block(a, b, at):
        frames, lanes = (1, 3) if a == 1 else (0, 2), 0 if a == 2 else 256
        cells = jnp.concatenate([xrows(f, b) for f in frames], axis=0)
        grad = mm(gt[:, lanes : lanes + 512], cells)
        for c in range(3):
            whole = grad[:, c * 128 : (c + 1) * 128].T
            mix[c, pl.ds(0, 128, stride=2), :] = whole[:, :128]
            mix[c, pl.ds(1, 128, stride=2), :] = whole[:, 128:]
            part[at + c * 256 : at + (c + 1) * 256, :] = mix[c].astype(BF)

    def dec_block(a, b, at):
        cells = jnp.concatenate([erows(a, b), erows(1 + a, b)], axis=0)
        grad = mm(st[...], cells)
        for c in range(3):
            part[at + c * 256 : at + (c + 1) * 256, :] = grad[c * 128 : (c + 1) * 128].T.astype(BF)

    sh = shards
    off = [sum(sh[:j]) for j in range(len(sh))]

    def grads(j):
        at = off[j] * n

        @pl.when(is_enc)
        def _():
            if CHUNKS[j][0] == (0, 0):
                collect(e_lg)
                gt[:, 512:768] = lg[2].reshape(256, 256).astype(F32).T.astype(BF)
            for i, (a, b) in enumerate(CHUNKS[j]):
                enc_block(a, b, at + i * BLOCK)

        @pl.when(jnp.logical_not(is_enc))
        def _():
            for i, (a, b) in enumerate(CHUNKS[j]):
                dec_block(a, b, at + i * BLOCK)

        used = BLOCK * len(CHUNKS[j])
        if n * sh[j] > used:
            part[at + used : at + n * sh[j], :] = jnp.zeros((n * sh[j] - used, 128), BF)

    def rows(start, count):
        return pl.ds(pl.multiple_of(start, 16), count)

    def move(src, dst, sems, i, to):
        return pltpu.make_async_remote_copy(
            src_ref=src,
            dst_ref=dst,
            send_sem=sems.at[0, i],
            recv_sem=sems.at[1, i],
            device_id=to,
            device_id_type=MESH,
        )

    sibling = (seg, k, s + 1 - 2 * core)
    sent = []

    def send(copy):
        copy.start()
        sent.append(copy)

    def arrived(dst, sems, i):
        move(dst, dst, sems, i, sibling).wait_recv()

    def at_y(p):
        return (seg, k, 2 * p + core)

    def half_of(ref, j):
        return ref.at[off[j] * n // 2 : off[j] * n // 2 + sh[j] * n // 2]

    def core_start(j):
        away = part.at[rows(off[j] * n + (1 - core) * (sh[j] * n // 2), sh[j] * n // 2)]
        send(move(away, half_of(rcv1, j), c_sem, j, sibling))

    def y_start(j):
        count = sh[j] * n // 2
        lo = off[j] * n // 2
        arrived(half_of(rcv1, j), c_sem, j)
        own = part[rows(off[j] * n + core * count, count), :].astype(F32)
        red1[lo : lo + count, :] = (own + rcv1[lo : lo + count, :].astype(F32)).astype(BF)
        for d in range(1, Y):
            p = (y + d) % Y
            i = j * (Y - 1) + d - 1
            slot = rcvy.at[d - 1, off[j] * T : (off[j] + sh[j]) * T]
            send(move(red1.at[rows(lo + p * T * sh[j], T * sh[j])], slot, y_sem, i, at_y(p)))

    def z_start(j):
        lo, count = off[j] * T, sh[j] * T
        total = red1[rows(off[j] * n // 2 + y * count, count), :].astype(F32)
        for d in range(1, Y):
            arrived(rcvy.at[d - 1, lo : lo + count], y_sem, j * (Y - 1) + d - 1)
            total = total + rcvy[d - 1, lo : lo + count, :].astype(F32)
        red2[lo : lo + count, :] = total.astype(BF)
        for d in range(1, T):
            p = (k + d) % T
            i = j * (T - 1) + d - 1
            slot = rcvz.at[d - 1, off[j] : off[j] + sh[j]]
            send(move(red2.at[rows(lo + p * sh[j], sh[j])], slot, z_sem, i, (seg, p, s)))

    def shard(j, py, pz):
        return rows(off[j] * n + ((core * Y + py) * T + pz) * sh[j], sh[j])

    def band(j, pc, py):
        return gat.at[rows(off[j] * n + (pc * Y + py) * T * sh[j], T * sh[j])]

    def gz_start(j):
        total = red2[rows(off[j] * T + k * sh[j], sh[j]), :].astype(F32)
        for d in range(1, T):
            arrived(rcvz.at[d - 1, off[j] : off[j] + sh[j]], z_sem, j * (T - 1) + d - 1)
            total = total + rcvz[d - 1, off[j] : off[j] + sh[j], :].astype(F32)
        mine = shard(j, y, k)
        gat[mine, :] = (total * scale).astype(BF)
        for d in range(1, T):
            send(move(gat.at[mine], gat.at[mine], gz_sem, j * (T - 1) + d - 1, (seg, (k + d) % T, s)))

    def gy_start(j):
        for d in range(1, T):
            arrived(gat.at[shard(j, y, (k - d + T) % T)], gz_sem, j * (T - 1) + d - 1)
        mine = band(j, core, y)
        for d in range(1, Y):
            send(move(mine, mine, gy_sem, j * (Y - 1) + d - 1, at_y((y + d) % Y)))
        send(move(mine, mine, gc_sem, j * Y, sibling))

    def gc_start(j):
        for d in range(1, Y):
            theirs = band(j, core, (y - d + Y) % Y)
            arrived(theirs, gy_sem, j * (Y - 1) + d - 1)
            send(move(theirs, theirs, gc_sem, j * Y + d, sibling))

    def written(j):
        copies = []
        for i, (a, b) in enumerate(CHUNKS[j]):
            src = gat.at[off[j] * n + i * BLOCK : off[j] * n + (i + 1) * BLOCK]
            dst = wout.at[(3 * a + b) * BLOCK : (3 * a + b + 1) * BLOCK]
            copies.append(pltpu.make_async_copy(src, dst, osem.at[1 + 3 * a + b]))
        return copies

    def finish(j):
        for d in range(Y):
            arrived(band(j, 1 - core, (y - d + Y) % Y), gc_sem, j * Y + d)
        for copy in written(j):
            copy.start()

    stages = [y_start, z_start, gz_start, gy_start, gc_start, finish]
    count = len(CHUNKS)
    for step in range(count + len(stages)):
        if step < count:
            grads(step)
            core_start(step)
        for j in range(count):
            if 0 <= step - j - 1 < len(stages):
                stages[step - j - 1](j)

    for copy in sent:
        copy.wait_send()

    @pl.when(is_enc)
    def _():
        drain(e_slope1)
        drain(e_slope0)
        drain(e_lg)

    drain(e_clip)
    drain(e_part)
    drain(e_lat1)
    drain(e_lat0)
    pltpu.make_async_copy(lg.at[pl.ds(0, 2)], latp, osem.at[0]).wait()
    for j in range(count):
        for copy in written(j):
            copy.wait()


def solution(mesh):
    T, S = mesh.shape["tm"], mesh.shape["space"]
    n = T * S
    shards = tuple(-(-len(blocks) * BLOCK // n // 16) * 16 for blocks in CHUNKS)
    sh = sum(shards)
    Y = S // 2
    half = n // 2 * sh
    count = len(CHUNKS)

    def on_device(clip_frames, enc_weight, dec_weight, out_grad):
        scale = 1.0 / math.sqrt(2 * 4 * 64 * n)
        dma = pltpu.SemaphoreType.DMA
        latp, wout = pl.pallas_call(
            functools.partial(kernel, T, S, shards, scale),
            out_shape=(
                jax.ShapeDtypeStruct((2, 4, 64, 256), BF),
                jax.ShapeDtypeStruct((9 * BLOCK, 128), BF),
            ),
            in_specs=[pl.BlockSpec(memory_space=pltpu.HBM)] * 4,
            out_specs=(pl.BlockSpec(memory_space=pl.ANY),) * 2,
            scratch_shapes=[
                pltpu.VMEM((4, 9, 128, 128), BF),
                pltpu.VMEM((4, 9, 64, 384), BF),
                pltpu.VMEM((9, 384, 256), BF),
                pltpu.VMEM((27, 256, 128), BF),
                pltpu.VMEM((2, 4, 64, 128), BF),
                pltpu.VMEM((256, 256), BF),
                pltpu.VMEM((256, 256), BF),
                pltpu.VMEM((4, 6, 64, 256), BF),
                pltpu.VMEM((4, 6, 64, 128), BF),
                pltpu.VMEM((4, 6, 64, 384), BF),
                pltpu.VMEM((3, 4, 64, 256), BF),
                pltpu.VMEM((256, 768), BF),
                pltpu.VMEM((384, 512), BF),
                pltpu.VMEM((3, 256, 128), F32),
                pltpu.VMEM((n * sh, 128), BF),
                pltpu.VMEM((half, 128), BF),
                pltpu.VMEM((half, 128), BF),
                pltpu.VMEM((Y - 1, T * sh, 128), BF),
                pltpu.VMEM((T * sh, 128), BF),
                pltpu.VMEM((T - 1, sh, 128), BF),
                pltpu.VMEM((n * sh, 128), BF),
                dma((4,)),
                dma((23,)),
                dma((23,)),
                dma((2, count)),
                dma((2, count * (Y - 1))),
                dma((2, count * (T - 1))),
                dma((2, count * (T - 1))),
                dma((2, count * (Y - 1))),
                dma((2, count * Y)),
                dma((10,)),
            ],
            compiler_params=pltpu.CompilerParams(
                collective_id=0, has_side_effects=True, vmem_limit_bytes=60 * 1024 * 1024
            ),
            cost_estimate=pl.CostEstimate(
                flops=5 * 10**9, bytes_accessed=12 * 10**6, transcendentals=65536
            ),
        )(
            clip_frames,
            enc_weight.reshape(9, 384, 256),
            dec_weight.reshape(27, 256, 128),
            out_grad,
        )
        flat = wout.reshape(1, TAPS, 32768).astype(F32)
        return latp[None], flat

    placed = (P("tm", "space", None, None), P(), P(), P("tm", "space", None, None))
    return jax.shard_map(
        on_device,
        mesh=mesh,
        in_specs=placed,
        out_specs=(P("segment", "tm", "space", None, None), P("segment", None, None)),
        check_vma=False,
    )
```

```python
import functools
import math

import jax
import jax.numpy as jnp
from jax import lax
from jax.experimental import pallas as pl
from jax.experimental.pallas import tpu as pltpu
from jax.sharding import PartitionSpec as P

MESH = pl.DeviceIdType.MESH
BF = jnp.bfloat16
F32 = jnp.float32
TAPS = 27
BLOCK = 3 * 256
CHUNKS = (
    ((2, 0), (2, 1), (2, 2)),
    ((0, 0), (0, 1), (0, 2)),
    ((1, 0), (1, 1), (1, 2)),
)


def mm(x, y):
    return jnp.dot(x, y, preferred_element_type=F32)


def kernel(
    T,
    S,
    shards,
    scale,
    clip,
    ew_h,
    dw_h,
    og_h,
    latp,
    wout,
    clipx,
    x3,
    ew,
    dw,
    dwt,
    og,
    pout,
    pin,
    ext,
    rim,
    s3,
    lg,
    gt,
    st,
    mix,
    part,
    rcv1,
    red1,
    rcvy,
    red2,
    rcvz,
    gat,
    lsem,
    ssem,
    rsem,
    c_sem,
    y_sem,
    z_sem,
    gz_sem,
    gy_sem,
    gc_sem,
    osem,
):
    seg = lax.axis_index("segment")
    k = lax.axis_index("tm")
    s = lax.axis_index("space")
    n = T * S
    Y = S // 2
    core = s % 2
    y = s // 2
    has_up, has_dn = s > 0, s < S - 1
    has_pv, has_nx = k > 0, k < T - 1
    is_enc = seg == 0

    loads = [
        pltpu.make_async_copy(clip, clipx.at[:, pl.ds(1, 8)], lsem.at[0]),
        pltpu.make_async_copy(ew_h, ew, lsem.at[1]),
        pltpu.make_async_copy(dw_h, dw, lsem.at[2]),
        pltpu.make_async_copy(og_h, og, lsem.at[3]),
    ]
    for c in loads:
        c.start()

    me = k * S + s
    barrier = pltpu.get_barrier_semaphore()

    def greet(d, carry):
        peer = (me + d) % n
        pl.semaphore_signal(
            barrier, inc=1, device_id=(seg, peer // S, peer % S), device_id_type=MESH
        )
        return carry

    lax.fori_loop(1, n, greet, 0)
    pl.semaphore_wait(barrier, n - 1)

    def remote(src, dst, i, to):
        return pltpu.make_async_remote_copy(
            src_ref=src,
            dst_ref=dst,
            send_sem=ssem.at[i],
            recv_sem=rsem.at[i],
            device_id=to,
            device_id_type=MESH,
        )

    def launch(entries):
        for copy, sends, gets, dst in entries:

            @pl.when(sends)
            def _():
                copy.start()

    def collect(entries):
        for copy, sends, gets, dst in entries:

            @pl.when(gets)
            def _():
                copy.wait_recv()

            @pl.when(jnp.logical_not(gets))
            def _():
                dst[...] = jnp.zeros(dst.shape, dst.dtype)

    def drain(entries):
        for copy, sends, gets, dst in entries:

            @pl.when(sends)
            def _():
                copy.wait_send()

    def entry(src, there, i, to, sends, gets):
        return (remote(src, there, i, to), sends, gets, there)

    e_clip = [
        entry(clip.at[:, pl.ds(7, 1)], clipx.at[:, pl.ds(0, 1)], 0, (seg, k, s + 1), has_dn, has_up)
    ]
    launch(e_clip)

    sel_i = lax.broadcasted_iota(jnp.int32, (192, 128), 0)
    sel_j = lax.broadcasted_iota(jnp.int32, (192, 128), 1)
    sel = (sel_j == 2 * (sel_i % 64) + sel_i // 64 - 1).astype(F32).astype(BF)

    def split_cols(f, r):
        y = mm(sel, clipx[f, r]).astype(BF)
        x3[f, r] = jnp.concatenate([y[:64], y[64:128], y[128:]], axis=1)

    loads[0].wait()

    def split_frame(f, carry):
        for r in range(1, 9):
            split_cols(f, r)
        return carry

    lax.fori_loop(0, 4, split_frame, 0)
    collect(e_clip)
    for f in range(4):
        split_cols(f, 0)
    loads[1].wait()

    def xrows(f, b):
        return jnp.concatenate([x3[f, b + 2 * h] for h in range(4)], axis=0)

    acc = jnp.zeros((256, 256), F32)
    for a in range(2):
        for b in range(3):
            acc = acc + mm(xrows(2 + a, b), ew[3 * a + b])
    pout[...] = acc.astype(BF)
    e_part = [entry(pout, pin, 1, (seg, k + 1, s), has_nx, has_pv)]
    launch(e_part)

    def lat_entries(f, base):
        own = 2 + f
        return [
            entry(ext.at[own, pl.ds(1, 4)], ext.at[f, pl.ds(1, 4)], base, (seg, k + 1, s), has_nx, has_pv),
            entry(ext.at[own, pl.ds(4, 1)], ext.at[own, pl.ds(0, 1)], base + 1, (seg, k, s + 1), has_dn, has_up),
            entry(ext.at[own, pl.ds(1, 1)], ext.at[own, pl.ds(5, 1)], base + 2, (seg, k, s - 1), has_up, has_dn),
            entry(
                ext.at[own, pl.ds(4, 1)],
                ext.at[f, pl.ds(0, 1)],
                base + 3,
                (seg, k + 1, s + 1),
                has_nx & has_dn,
                has_pv & has_up,
            ),
            entry(
                ext.at[own, pl.ds(1, 1)],
                ext.at[f, pl.ds(5, 1)],
                base + 4,
                (seg, k + 1, s - 1),
                has_nx & has_up,
                has_pv & has_dn,
            ),
        ]

    acc = jnp.zeros((256, 256), F32)
    for a in range(3):
        for b in range(3):
            acc = acc + mm(xrows(a, b), ew[3 * a + b])
    ext[3, 1:5] = acc.astype(BF).reshape(4, 64, 256)
    e_lat1 = lat_entries(1, 2)
    launch(e_lat1)

    acc = jnp.zeros((256, 256), F32)
    for b in range(3):
        acc = acc + mm(xrows(0, b), ew[6 + b])
    loads[2].wait()
    loads[3].wait()

    def turn(ab, carry):
        for c in range(3):
            dwt[ab, c * 128 : (c + 1) * 128, :] = dw[3 * ab + c].astype(F32).T.astype(BF)
        return carry

    @pl.when(is_enc)
    def _():
        lax.fori_loop(0, 4, turn, 0)

    collect(e_part)
    ext[2, 1:5] = (acc + pin[...].astype(F32)).astype(BF).reshape(4, 64, 256)
    e_lat0 = lat_entries(0, 7)
    launch(e_lat0)

    @pl.when(is_enc)
    def _():
        lax.fori_loop(4, 9, turn, 0)

    col = lax.broadcasted_iota(jnp.int32, (256, 128), 0) % 64

    def dcat(ab):
        return jnp.concatenate([dw[3 * ab], dw[3 * ab + 1], dw[3 * ab + 2]], axis=1)

    def erows(f, b):
        return jnp.concatenate([ext[f, b + h] for h in range(4)], axis=0)

    def decode(acc, t, taps_t):
        for a in taps_t:
            for b in range(3):
                acc = acc + mm(erows(t + a, b), dcat(3 * a + b))
        return acc

    def slope_of(acc, t):
        before = jnp.where(col == 0, 0.0, pltpu.roll(acc[:, :128], 1, 0))
        after = jnp.where(col == 63, 0.0, pltpu.roll(acc[:, 256:], 255, 0))
        pre = before + acc[:, 128:256] + after
        sg = jax.nn.sigmoid(pre)
        slope = og[t].reshape(256, 128).astype(F32) * sg * (1.0 + pre * (1.0 - sg))
        rim[t, 1:5] = slope.astype(BF).reshape(4, 64, 128)

    def slope_entries(f, base):
        own = rim.at[f, pl.ds(1, 4)]
        top = rim.at[f, pl.ds(1, 1)]
        last = rim.at[f, pl.ds(4, 1)]
        far = 2 + f
        return [
            entry(own, rim.at[far, pl.ds(1, 4)], base, (seg, k - 1, s), has_pv, has_nx),
            entry(last, rim.at[f, pl.ds(0, 1)], base + 1, (seg, k, s + 1), has_dn, has_up),
            entry(top, rim.at[f, pl.ds(5, 1)], base + 2, (seg, k, s - 1), has_up, has_dn),
            entry(last, rim.at[far, pl.ds(0, 1)], base + 3, (seg, k - 1, s + 1), has_pv & has_dn, has_nx & has_up),
            entry(top, rim.at[far, pl.ds(5, 1)], base + 4, (seg, k - 1, s - 1), has_pv & has_up, has_nx & has_dn),
        ]

    e_slope1 = slope_entries(1, 12)
    e_slope0 = slope_entries(0, 17)
    e_lg = [entry(lg.at[0], lg.at[2], 22, (seg, k - 1, s), has_pv, has_nx)]

    collect(e_lat1[1:3])
    collect(e_lat0[1:3])
    zero = jnp.zeros((256, 384), F32)
    acc1 = decode(zero, 1, (1, 2))
    acc0 = decode(zero, 0, (2,))
    collect(e_lat1[:1] + e_lat1[3:])
    slope_of(decode(acc1, 1, (0,)), 1)

    @pl.when(is_enc)
    def _():
        launch(e_slope1)

    acc0 = decode(acc0, 0, (1,))
    collect(e_lat0[:1] + e_lat0[3:])
    slope_of(decode(acc0, 0, (0,)), 0)

    @pl.when(is_enc)
    def _():
        launch(e_slope0)

    col64 = lax.broadcasted_iota(jnp.int32, (64, 128), 0)

    def shifts(v):
        later = jnp.where(col64 == 63, 0.0, pltpu.roll(v, 63, 0))
        sooner = jnp.where(col64 == 0, 0.0, pltpu.roll(v, 1, 0))
        return jnp.concatenate([later, v, sooner], axis=1)

    def put_shifts(f, which):
        for r in which:
            s3[f, r] = shifts(rim[f, r].astype(F32)).astype(BF)

    def transpose(acc, t, taps_t):
        for a in taps_t:
            for b in range(3):
                cells = jnp.concatenate([s3[t + 2 - a, h + 2 - b] for h in range(4)], axis=0)
                acc = acc + mm(cells, dwt[3 * a + b])
        return acc

    def keep(acc, t):
        rounded = acc.astype(BF)
        lg[t] = rounded.reshape(4, 64, 256)
        if t == 0:
            launch(e_lg)
        gt[:, t * 256 : (t + 1) * 256] = rounded.astype(F32).T.astype(BF)

    @pl.when(is_enc)
    def _():
        for f in (1, 0):
            put_shifts(f, range(1, 5))
        collect(e_slope1[1:3])
        collect(e_slope0[1:3])
        for f in (1, 0):
            put_shifts(f, (0, 5))
        zero = jnp.zeros((256, 256), F32)
        acc0 = transpose(zero, 0, (1, 2))
        acc1 = transpose(zero, 1, (2,))
        collect(e_slope1[:1] + e_slope1[3:])
        put_shifts(3, range(6))
        collect(e_slope0[:1] + e_slope0[3:])
        put_shifts(2, range(6))
        keep(transpose(acc0, 0, (0,)), 0)
        keep(transpose(acc1, 1, (0, 1)), 1)
        pltpu.make_async_copy(lg.at[pl.ds(0, 2)], latp, osem.at[0]).start()

    @pl.when(jnp.logical_not(is_enc))
    def _():
        pltpu.make_async_copy(ext.at[pl.ds(2, 2), pl.ds(1, 4)], latp, osem.at[0]).start()
        for t in range(2):
            cells = jnp.concatenate([shifts(rim[t, 1 + h].astype(F32)) for h in range(4)], axis=0)
            st[:, t * 256 : (t + 1) * 256] = cells.T.astype(BF)

    def enc_block(a, b, at):
        frames, lanes = (1, 3) if a == 1 else (0, 2), 0 if a == 2 else 256
        cells = jnp.concatenate([xrows(f, b) for f in frames], axis=0)
        grad = mm(gt[:, lanes : lanes + 512], cells)
        for c in range(3):
            whole = grad[:, c * 128 : (c + 1) * 128].T
            mix[c, pl.ds(0, 128, stride=2), :] = whole[:, :128]
            mix[c, pl.ds(1, 128, stride=2), :] = whole[:, 128:]
            part[at + c * 256 : at + (c + 1) * 256, :] = mix[c].astype(BF)

    def dec_block(a, b, at):
        cells = jnp.concatenate([erows(a, b), erows(1 + a, b)], axis=0)
        grad = mm(st[...], cells)
        for c in range(3):
            part[at + c * 256 : at + (c + 1) * 256, :] = grad[c * 128 : (c + 1) * 128].T.astype(BF)

    sh = shards
    off = [sum(sh[:j]) for j in range(len(sh))]

    def grads(j):
        at = off[j] * n

        @pl.when(is_enc)
        def _():
            if CHUNKS[j][0] == (0, 0):
                collect(e_lg)
                gt[:, 512:768] = lg[2].reshape(256, 256).astype(F32).T.astype(BF)
            for i, (a, b) in enumerate(CHUNKS[j]):
                enc_block(a, b, at + i * BLOCK)

        @pl.when(jnp.logical_not(is_enc))
        def _():
            for i, (a, b) in enumerate(CHUNKS[j]):
                dec_block(a, b, at + i * BLOCK)

        used = BLOCK * len(CHUNKS[j])
        if n * sh[j] > used:
            part[at + used : at + n * sh[j], :] = jnp.zeros((n * sh[j] - used, 128), BF)

    def rows(start, count):
        return pl.ds(pl.multiple_of(start, 16), count)

    def move(src, dst, sems, i, to):
        return pltpu.make_async_remote_copy(
            src_ref=src,
            dst_ref=dst,
            send_sem=sems.at[0, i],
            recv_sem=sems.at[1, i],
            device_id=to,
            device_id_type=MESH,
        )

    sibling = (seg, k, s + 1 - 2 * core)
    sent = []

    def send(copy):
        copy.start()
        sent.append(copy)

    def arrived(dst, sems, i):
        move(dst, dst, sems, i, sibling).wait_recv()

    def at_y(p):
        return (seg, k, 2 * p + core)

    def half_of(ref, j):
        return ref.at[off[j] * n // 2 : off[j] * n // 2 + sh[j] * n // 2]

    def core_start(j):
        away = part.at[rows(off[j] * n + (1 - core) * (sh[j] * n // 2), sh[j] * n // 2)]
        send(move(away, half_of(rcv1, j), c_sem, j, sibling))

    def y_start(j):
        count = sh[j] * n // 2
        lo = off[j] * n // 2
        arrived(half_of(rcv1, j), c_sem, j)
        own = part[rows(off[j] * n + core * count, count), :].astype(F32)
        red1[lo : lo + count, :] = (own + rcv1[lo : lo + count, :].astype(F32)).astype(BF)
        for d in range(1, Y):
            p = (y + d) % Y
            i = j * (Y - 1) + d - 1
            slot = rcvy.at[d - 1, off[j] * T : (off[j] + sh[j]) * T]
            send(move(red1.at[rows(lo + p * T * sh[j], T * sh[j])], slot, y_sem, i, at_y(p)))

    def z_start(j):
        lo, count = off[j] * T, sh[j] * T
        total = red1[rows(off[j] * n // 2 + y * count, count), :].astype(F32)
        for d in range(1, Y):
            arrived(rcvy.at[d - 1, lo : lo + count], y_sem, j * (Y - 1) + d - 1)
            total = total + rcvy[d - 1, lo : lo + count, :].astype(F32)
        red2[lo : lo + count, :] = total.astype(BF)
        for d in range(1, T):
            p = (k + d) % T
            i = j * (T - 1) + d - 1
            slot = rcvz.at[d - 1, off[j] : off[j] + sh[j]]
            send(move(red2.at[rows(lo + p * sh[j], sh[j])], slot, z_sem, i, (seg, p, s)))

    def shard(j, py, pz):
        return rows(off[j] * n + ((core * Y + py) * T + pz) * sh[j], sh[j])

    def band(j, pc, py):
        return gat.at[rows(off[j] * n + (pc * Y + py) * T * sh[j], T * sh[j])]

    def gz_start(j):
        total = red2[rows(off[j] * T + k * sh[j], sh[j]), :].astype(F32)
        for d in range(1, T):
            arrived(rcvz.at[d - 1, off[j] : off[j] + sh[j]], z_sem, j * (T - 1) + d - 1)
            total = total + rcvz[d - 1, off[j] : off[j] + sh[j], :].astype(F32)
        mine = shard(j, y, k)
        gat[mine, :] = (total * scale).astype(BF)
        for d in range(1, T):
            send(move(gat.at[mine], gat.at[mine], gz_sem, j * (T - 1) + d - 1, (seg, (k + d) % T, s)))

    def gy_start(j):
        for d in range(1, T):
            arrived(gat.at[shard(j, y, (k - d + T) % T)], gz_sem, j * (T - 1) + d - 1)
        mine = band(j, core, y)
        for d in range(1, Y):
            send(move(mine, mine, gy_sem, j * (Y - 1) + d - 1, at_y((y + d) % Y)))
        send(move(mine, mine, gc_sem, j * Y, sibling))

    def gc_start(j):
        for d in range(1, Y):
            theirs = band(j, core, (y - d + Y) % Y)
            arrived(theirs, gy_sem, j * (Y - 1) + d - 1)
            send(move(theirs, theirs, gc_sem, j * Y + d, sibling))

    def written(j):
        copies = []
        for i, (a, b) in enumerate(CHUNKS[j]):
            src = gat.at[off[j] * n + i * BLOCK : off[j] * n + (i + 1) * BLOCK]
            dst = wout.at[(3 * a + b) * BLOCK : (3 * a + b + 1) * BLOCK]
            copies.append(pltpu.make_async_copy(src, dst, osem.at[1 + 3 * a + b]))
        return copies

    def finish(j):
        for d in range(Y):
            arrived(band(j, 1 - core, (y - d + Y) % Y), gc_sem, j * Y + d)
        for copy in written(j):
            copy.start()

    stages = [y_start, z_start, gz_start, gy_start, gc_start, finish]
    count = len(CHUNKS)
    for step in range(count + len(stages)):
        if step < count:
            grads(step)
            core_start(step)
        for j in range(count):
            if 0 <= step - j - 1 < len(stages):
                stages[step - j - 1](j)

    for copy in sent:
        copy.wait_send()

    @pl.when(is_enc)
    def _():
        drain(e_slope1)
        drain(e_slope0)
        drain(e_lg)

    drain(e_clip)
    drain(e_part)
    drain(e_lat1)
    drain(e_lat0)
    pltpu.make_async_copy(lg.at[pl.ds(0, 2)], latp, osem.at[0]).wait()
    for j in range(count):
        for copy in written(j):
            copy.wait()


def solution(mesh):
    T, S = mesh.shape["tm"], mesh.shape["space"]
    n = T * S
    shards = tuple(-(-len(blocks) * BLOCK // n // 16) * 16 for blocks in CHUNKS)
    sh = sum(shards)
    Y = S // 2
    half = n // 2 * sh
    count = len(CHUNKS)

    def on_device(clip_frames, enc_weight, dec_weight, out_grad):
        scale = 1.0 / math.sqrt(2 * 4 * 64 * n)
        dma = pltpu.SemaphoreType.DMA
        latp, wout = pl.pallas_call(
            functools.partial(kernel, T, S, shards, scale),
            out_shape=(
                jax.ShapeDtypeStruct((2, 4, 64, 256), BF),
                jax.ShapeDtypeStruct((9 * BLOCK, 128), BF),
            ),
            in_specs=[pl.BlockSpec(memory_space=pltpu.HBM)] * 4,
            out_specs=(pl.BlockSpec(memory_space=pl.ANY),) * 2,
            scratch_shapes=[
                pltpu.VMEM((4, 9, 128, 128), BF),
                pltpu.VMEM((4, 9, 64, 384), BF),
                pltpu.VMEM((9, 384, 256), BF),
                pltpu.VMEM((27, 256, 128), BF),
                pltpu.VMEM((9, 384, 256), BF),
                pltpu.VMEM((2, 4, 64, 128), BF),
                pltpu.VMEM((256, 256), BF),
                pltpu.VMEM((256, 256), BF),
                pltpu.VMEM((4, 6, 64, 256), BF),
                pltpu.VMEM((4, 6, 64, 128), BF),
                pltpu.VMEM((4, 6, 64, 384), BF),
                pltpu.VMEM((3, 4, 64, 256), BF),
                pltpu.VMEM((256, 768), BF),
                pltpu.VMEM((384, 512), BF),
                pltpu.VMEM((3, 256, 128), F32),
                pltpu.VMEM((n * sh, 128), BF),
                pltpu.VMEM((half, 128), BF),
                pltpu.VMEM((half, 128), BF),
                pltpu.VMEM((Y - 1, T * sh, 128), BF),
                pltpu.VMEM((T * sh, 128), BF),
                pltpu.VMEM((T - 1, sh, 128), BF),
                pltpu.VMEM((n * sh, 128), BF),
                dma((4,)),
                dma((23,)),
                dma((23,)),
                dma((2, count)),
                dma((2, count * (Y - 1))),
                dma((2, count * (T - 1))),
                dma((2, count * (T - 1))),
                dma((2, count * (Y - 1))),
                dma((2, count * Y)),
                dma((10,)),
            ],
            compiler_params=pltpu.CompilerParams(
                collective_id=0, has_side_effects=True, vmem_limit_bytes=60 * 1024 * 1024
            ),
            cost_estimate=pl.CostEstimate(
                flops=5 * 10**9, bytes_accessed=12 * 10**6, transcendentals=65536
            ),
        )(
            clip_frames,
            enc_weight.reshape(9, 384, 256),
            dec_weight.reshape(27, 256, 128),
            out_grad,
        )
        flat = wout.reshape(1, TAPS, 32768).astype(F32)
        return latp[None], flat

    placed = (P("tm", "space", None, None), P(), P(), P("tm", "space", None, None))
    return jax.shard_map(
        on_device,
        mesh=mesh,
        in_specs=placed,
        out_specs=(P("segment", "tm", "space", None, None), P("segment", None, None)),
        check_vma=False,
    )
```

```python
import functools
import math

import jax
import jax.numpy as jnp
from jax import lax
from jax.experimental import pallas as pl
from jax.experimental.pallas import tpu as pltpu
from jax.sharding import PartitionSpec as P

MESH = pl.DeviceIdType.MESH
BF = jnp.bfloat16
F32 = jnp.float32
TAPS = 27
BLOCK = 3 * 256
CHUNKS = (
    ((2, 0), (2, 1), (2, 2)),
    ((0, 0), (0, 1), (0, 2)),
    ((1, 0), (1, 1), (1, 2)),
)


def mm(x, y):
    return jnp.dot(x, y, preferred_element_type=F32)


def widen(narrow, wide):
    wide[...] = narrow[...].astype(F32)


def kernel(
    T,
    S,
    shards,
    scale,
    clip,
    ew_h,
    dw_h,
    og_h,
    latp,
    wout,
    clipx,
    x3,
    ew,
    dw,
    dwt,
    og,
    pout,
    pin,
    ext,
    rim,
    s3,
    lg,
    gt,
    st,
    mix,
    part,
    rcv1,
    red1,
    rcvy,
    red2,
    rcvz,
    gat,
    lsem,
    ssem,
    rsem,
    c_sem,
    y_sem,
    z_sem,
    gz_sem,
    gy_sem,
    gc_sem,
    osem,
):
    seg = lax.axis_index("segment")
    k = lax.axis_index("tm")
    s = lax.axis_index("space")
    n = T * S
    Y = S // 2
    core = s % 2
    y = s // 2
    has_up, has_dn = s > 0, s < S - 1
    has_pv, has_nx = k > 0, k < T - 1
    is_enc = seg == 0

    loads = [
        pltpu.make_async_copy(clip.at[pl.ds(2, 2)], clipx.at[pl.ds(2, 2), pl.ds(1, 8)], lsem.at[0]),
        pltpu.make_async_copy(ew_h, ew, lsem.at[1]),
        pltpu.make_async_copy(dw_h, dw, lsem.at[2]),
        pltpu.make_async_copy(og_h, og, lsem.at[3]),
        pltpu.make_async_copy(clip.at[pl.ds(0, 2)], clipx.at[pl.ds(0, 2), pl.ds(1, 8)], lsem.at[4]),
    ]
    for i in (0, 1, 4, 2, 3):
        loads[i].start()

    me = k * S + s
    barrier = pltpu.get_barrier_semaphore()

    def greet(d, carry):
        peer = (me + d) % n
        pl.semaphore_signal(
            barrier, inc=1, device_id=(seg, peer // S, peer % S), device_id_type=MESH
        )
        return carry

    lax.fori_loop(1, n, greet, 0)
    pl.semaphore_wait(barrier, n - 1)

    def remote(src, dst, i, to):
        return pltpu.make_async_remote_copy(
            src_ref=src,
            dst_ref=dst,
            send_sem=ssem.at[i],
            recv_sem=rsem.at[i],
            device_id=to,
            device_id_type=MESH,
        )

    def launch(entries):
        for copy, sends, gets, dst in entries:

            @pl.when(sends)
            def _():
                copy.start()

    def collect(entries):
        for copy, sends, gets, dst in entries:

            @pl.when(gets)
            def _():
                copy.wait_recv()

            @pl.when(jnp.logical_not(gets))
            def _():
                dst[...] = jnp.zeros(dst.shape, dst.dtype)

    def drain(entries):
        for copy, sends, gets, dst in entries:

            @pl.when(sends)
            def _():
                copy.wait_send()

    def entry(src, there, i, to, sends, gets):
        return (remote(src, there, i, to), sends, gets, there)

    def clip_entry(f, i):
        src = clip.at[pl.ds(f, 2), pl.ds(7, 1)]
        return entry(src, clipx.at[pl.ds(f, 2), pl.ds(0, 1)], i, (seg, k, s + 1), has_dn, has_up)

    e_clip = [clip_entry(2, 0), clip_entry(0, 23)]
    launch(e_clip)

    sel_i = lax.broadcasted_iota(jnp.int32, (192, 128), 0)
    sel_j = lax.broadcasted_iota(jnp.int32, (192, 128), 1)
    sel = (sel_j == 2 * (sel_i % 64) + sel_i // 64 - 1).astype(F32).astype(BF)

    def split_cols(f, r):
        y = mm(sel, clipx[f, r]).astype(BF)
        x3[f, r] = jnp.concatenate([y[:64], y[64:128], y[128:]], axis=1)

    def split_frame(f, carry):
        for r in range(1, 9):
            split_cols(f, r)
        return carry

    loads[0].wait()
    lax.fori_loop(2, 4, split_frame, 0)
    collect(e_clip[:1])
    for f in range(2, 4):
        split_cols(f, 0)
    loads[1].wait()

    def xrows(f, b):
        return jnp.concatenate([x3[f, b + 2 * h] for h in range(4)], axis=0)

    acc = jnp.zeros((256, 256), F32)
    for a in range(2):
        for b in range(3):
            acc = acc + mm(xrows(2 + a, b), ew[3 * a + b])
    pout[...] = acc.astype(BF)
    e_part = [entry(pout, pin, 1, (seg, k + 1, s), has_nx, has_pv)]
    launch(e_part)
    loads[4].wait()
    lax.fori_loop(0, 2, split_frame, 0)
    collect(e_clip[1:])
    for f in range(2):
        split_cols(f, 0)

    def lat_entries(f, base):
        own = 2 + f
        return [
            entry(ext.at[own, pl.ds(1, 4)], ext.at[f, pl.ds(1, 4)], base, (seg, k + 1, s), has_nx, has_pv),
            entry(ext.at[own, pl.ds(4, 1)], ext.at[own, pl.ds(0, 1)], base + 1, (seg, k, s + 1), has_dn, has_up),
            entry(ext.at[own, pl.ds(1, 1)], ext.at[own, pl.ds(5, 1)], base + 2, (seg, k, s - 1), has_up, has_dn),
            entry(
                ext.at[own, pl.ds(4, 1)],
                ext.at[f, pl.ds(0, 1)],
                base + 3,
                (seg, k + 1, s + 1),
                has_nx & has_dn,
                has_pv & has_up,
            ),
            entry(
                ext.at[own, pl.ds(1, 1)],
                ext.at[f, pl.ds(5, 1)],
                base + 4,
                (seg, k + 1, s - 1),
                has_nx & has_up,
                has_pv & has_dn,
            ),
        ]

    acc = jnp.zeros((256, 256), F32)
    for a in range(3):
        for b in range(3):
            acc = acc + mm(xrows(a, b), ew[3 * a + b])
    ext[3, 1:5] = acc.astype(BF).reshape(4, 64, 256)
    e_lat1 = lat_entries(1, 2)
    launch(e_lat1)

    acc = jnp.zeros((256, 256), F32)
    for b in range(3):
        acc = acc + mm(xrows(0, b), ew[6 + b])
    loads[2].wait()
    loads[3].wait()

    def turn(ab, carry):
        for c in range(3):
            dwt[ab, c * 128 : (c + 1) * 128, :] = dw[3 * ab + c].astype(F32).T.astype(BF)
        return carry

    @pl.when(is_enc)
    def _():
        lax.fori_loop(0, 4, turn, 0)

    collect(e_part)
    ext[2, 1:5] = (acc + pin[...].astype(F32)).astype(BF).reshape(4, 64, 256)
    e_lat0 = lat_entries(0, 7)
    launch(e_lat0)

    @pl.when(is_enc)
    def _():
        lax.fori_loop(4, 9, turn, 0)

    col = lax.broadcasted_iota(jnp.int32, (256, 128), 0) % 64

    def dcat(ab):
        return jnp.concatenate([dw[3 * ab], dw[3 * ab + 1], dw[3 * ab + 2]], axis=1)

    def erows(f, b):
        return jnp.concatenate([ext[f, b + h] for h in range(4)], axis=0)

    def decode(acc, t, taps_t):
        for a in taps_t:
            for b in range(3):
                acc = acc + mm(erows(t + a, b), dcat(3 * a + b))
        return acc

    def slope_of(acc, t):
        before = jnp.where(col == 0, 0.0, pltpu.roll(acc[:, :128], 1, 0))
        after = jnp.where(col == 63, 0.0, pltpu.roll(acc[:, 256:], 255, 0))
        pre = before + acc[:, 128:256] + after
        sg = jax.nn.sigmoid(pre)
        slope = og[t].reshape(256, 128).astype(F32) * sg * (1.0 + pre * (1.0 - sg))
        rim[t, 1:5] = slope.astype(BF).reshape(4, 64, 128)

    def slope_entries(f, base):
        own = rim.at[f, pl.ds(1, 4)]
        top = rim.at[f, pl.ds(1, 1)]
        last = rim.at[f, pl.ds(4, 1)]
        far = 2 + f
        return [
            entry(own, rim.at[far, pl.ds(1, 4)], base, (seg, k - 1, s), has_pv, has_nx),
            entry(last, rim.at[f, pl.ds(0, 1)], base + 1, (seg, k, s + 1), has_dn, has_up),
            entry(top, rim.at[f, pl.ds(5, 1)], base + 2, (seg, k, s - 1), has_up, has_dn),
            entry(last, rim.at[far, pl.ds(0, 1)], base + 3, (seg, k - 1, s + 1), has_pv & has_dn, has_nx & has_up),
            entry(top, rim.at[far, pl.ds(5, 1)], base + 4, (seg, k - 1, s - 1), has_pv & has_up, has_nx & has_dn),
        ]

    e_slope1 = slope_entries(1, 12)
    e_slope0 = slope_entries(0, 17)
    e_lg = [entry(lg.at[0], lg.at[2], 22, (seg, k - 1, s), has_pv, has_nx)]

    collect(e_lat1[1:3])
    collect(e_lat0[1:3])
    zero = jnp.zeros((256, 384), F32)
    acc1 = decode(zero, 1, (1, 2))
    acc0 = decode(zero, 0, (2,))
    collect(e_lat1[:1] + e_lat1[3:])
    slope_of(decode(acc1, 1, (0,)), 1)

    @pl.when(is_enc)
    def _():
        launch(e_slope1)

    acc0 = decode(acc0, 0, (1,))
    collect(e_lat0[:1] + e_lat0[3:])
    slope_of(decode(acc0, 0, (0,)), 0)

    @pl.when(is_enc)
    def _():
        launch(e_slope0)

    col64 = lax.broadcasted_iota(jnp.int32, (64, 128), 0)

    def shifts(v):
        later = jnp.where(col64 == 63, 0.0, pltpu.roll(v, 63, 0))
        sooner = jnp.where(col64 == 0, 0.0, pltpu.roll(v, 1, 0))
        return jnp.concatenate([later, v, sooner], axis=1)

    def put_shifts(f, which):
        for r in which:
            s3[f, r] = shifts(rim[f, r].astype(F32)).astype(BF)

    def transpose(acc, t, taps_t):
        for a in taps_t:
            for b in range(3):
                cells = jnp.concatenate([s3[t + 2 - a, h + 2 - b] for h in range(4)], axis=0)
                acc = acc + mm(cells, dwt[3 * a + b])
        return acc

    def keep(acc, t):
        rounded = acc.astype(BF)
        lg[t] = rounded.reshape(4, 64, 256)
        if t == 0:
            launch(e_lg)
        gt[:, t * 256 : (t + 1) * 256] = rounded.astype(F32).T.astype(BF)

    @pl.when(is_enc)
    def _():
        for f in (1, 0):
            put_shifts(f, range(1, 5))
        collect(e_slope1[1:3])
        collect(e_slope0[1:3])
        for f in (1, 0):
            put_shifts(f, (0, 5))
        zero = jnp.zeros((256, 256), F32)
        acc0 = transpose(zero, 0, (1, 2))
        acc1 = transpose(zero, 1, (2,))
        collect(e_slope1[:1] + e_slope1[3:])
        put_shifts(3, range(6))
        collect(e_slope0[:1] + e_slope0[3:])
        put_shifts(2, range(6))
        keep(transpose(acc0, 0, (0,)), 0)
        keep(transpose(acc1, 1, (0, 1)), 1)
        pltpu.make_async_copy(lg.at[pl.ds(0, 2)], latp, osem.at[0]).start()

    @pl.when(jnp.logical_not(is_enc))
    def _():
        pltpu.make_async_copy(ext.at[pl.ds(2, 2), pl.ds(1, 4)], latp, osem.at[0]).start()
        for t in range(2):
            cells = jnp.concatenate([shifts(rim[t, 1 + h].astype(F32)) for h in range(4)], axis=0)
            st[:, t * 256 : (t + 1) * 256] = cells.T.astype(BF)

    def enc_block(a, b, at):
        frames, lanes = (1, 3) if a == 1 else (0, 2), 0 if a == 2 else 256
        cells = jnp.concatenate([xrows(f, b) for f in frames], axis=0)
        grad = mm(gt[:, lanes : lanes + 512], cells)
        for c in range(3):
            whole = grad[:, c * 128 : (c + 1) * 128].T
            mix[c, pl.ds(0, 128, stride=2), :] = whole[:, :128]
            mix[c, pl.ds(1, 128, stride=2), :] = whole[:, 128:]
            part[at + c * 256 : at + (c + 1) * 256, :] = mix[c].astype(BF)

    def dec_block(a, b, at):
        cells = jnp.concatenate([erows(a, b), erows(1 + a, b)], axis=0)
        grad = mm(st[...], cells)
        for c in range(3):
            part[at + c * 256 : at + (c + 1) * 256, :] = grad[c * 128 : (c + 1) * 128].T.astype(BF)

    sh = shards
    off = [sum(sh[:j]) for j in range(len(sh))]

    def grads(j):
        at = off[j] * n

        @pl.when(is_enc)
        def _():
            if CHUNKS[j][0] == (0, 0):
                collect(e_lg)
                gt[:, 512:768] = lg[2].reshape(256, 256).astype(F32).T.astype(BF)
            for i, (a, b) in enumerate(CHUNKS[j]):
                enc_block(a, b, at + i * BLOCK)

        @pl.when(jnp.logical_not(is_enc))
        def _():
            for i, (a, b) in enumerate(CHUNKS[j]):
                dec_block(a, b, at + i * BLOCK)

        used = BLOCK * len(CHUNKS[j])
        if n * sh[j] > used:
            part[at + used : at + n * sh[j], :] = jnp.zeros((n * sh[j] - used, 128), BF)

    def rows(start, count):
        return pl.ds(pl.multiple_of(start, 16), count)

    def move(src, dst, sems, i, to):
        return pltpu.make_async_remote_copy(
            src_ref=src,
            dst_ref=dst,
            send_sem=sems.at[0, i],
            recv_sem=sems.at[1, i],
            device_id=to,
            device_id_type=MESH,
        )

    sibling = (seg, k, s + 1 - 2 * core)
    sent = []

    def send(copy):
        copy.start()
        sent.append(copy)

    def arrived(dst, sems, i):
        move(dst, dst, sems, i, sibling).wait_recv()

    def at_y(p):
        return (seg, k, 2 * p + core)

    def half_of(ref, j):
        return ref.at[off[j] * n // 2 : off[j] * n // 2 + sh[j] * n // 2]

    def core_start(j):
        away = part.at[rows(off[j] * n + (1 - core) * (sh[j] * n // 2), sh[j] * n // 2)]
        send(move(away, half_of(rcv1, j), c_sem, j, sibling))

    def y_start(j):
        count = sh[j] * n // 2
        lo = off[j] * n // 2
        arrived(half_of(rcv1, j), c_sem, j)
        own = part[rows(off[j] * n + core * count, count), :].astype(F32)
        red1[lo : lo + count, :] = (own + rcv1[lo : lo + count, :].astype(F32)).astype(BF)
        for d in range(1, Y):
            p = (y + d) % Y
            i = j * (Y - 1) + d - 1
            slot = rcvy.at[d - 1, off[j] * T : (off[j] + sh[j]) * T]
            send(move(red1.at[rows(lo + p * T * sh[j], T * sh[j])], slot, y_sem, i, at_y(p)))

    def z_start(j):
        lo, count = off[j] * T, sh[j] * T
        total = red1[rows(off[j] * n // 2 + y * count, count), :].astype(F32)
        for d in range(1, Y):
            arrived(rcvy.at[d - 1, lo : lo + count], y_sem, j * (Y - 1) + d - 1)
            total = total + rcvy[d - 1, lo : lo + count, :].astype(F32)
        red2[lo : lo + count, :] = total.astype(BF)
        for d in range(1, T):
            p = (k + d) % T
            i = j * (T - 1) + d - 1
            slot = rcvz.at[d - 1, off[j] : off[j] + sh[j]]
            send(move(red2.at[rows(lo + p * sh[j], sh[j])], slot, z_sem, i, (seg, p, s)))

    def shard(j, py, pz):
        return rows(off[j] * n + ((core * Y + py) * T + pz) * sh[j], sh[j])

    def band(j, pc, py):
        return gat.at[rows(off[j] * n + (pc * Y + py) * T * sh[j], T * sh[j])]

    def gz_start(j):
        total = red2[rows(off[j] * T + k * sh[j], sh[j]), :].astype(F32)
        for d in range(1, T):
            arrived(rcvz.at[d - 1, off[j] : off[j] + sh[j]], z_sem, j * (T - 1) + d - 1)
            total = total + rcvz[d - 1, off[j] : off[j] + sh[j], :].astype(F32)
        mine = shard(j, y, k)
        gat[mine, :] = (total * scale).astype(BF)
        for d in range(1, T):
            send(move(gat.at[mine], gat.at[mine], gz_sem, j * (T - 1) + d - 1, (seg, (k + d) % T, s)))

    def gy_start(j):
        for d in range(1, T):
            arrived(gat.at[shard(j, y, (k - d + T) % T)], gz_sem, j * (T - 1) + d - 1)
        mine = band(j, core, y)
        for d in range(1, Y):
            send(move(mine, mine, gy_sem, j * (Y - 1) + d - 1, at_y((y + d) % Y)))
        send(move(mine, mine, gc_sem, j * Y, sibling))

    def gc_start(j):
        for d in range(1, Y):
            theirs = band(j, core, (y - d + Y) % Y)
            arrived(theirs, gy_sem, j * (Y - 1) + d - 1)
            send(move(theirs, theirs, gc_sem, j * Y + d, sibling))

    def written(j):
        copies = []
        for i, (a, b) in enumerate(CHUNKS[j]):
            src = gat.at[off[j] * n + i * BLOCK : off[j] * n + (i + 1) * BLOCK]
            dst = wout.at[(3 * a + b) * BLOCK : (3 * a + b + 1) * BLOCK]
            copies.append(pltpu.make_async_copy(src, dst, osem.at[1 + 3 * a + b]))
        return copies

    def finish(j):
        for d in range(Y):
            arrived(band(j, 1 - core, (y - d + Y) % Y), gc_sem, j * Y + d)
        for copy in written(j):
            copy.start()

    stages = [y_start, z_start, gz_start, gy_start, gc_start, finish]
    count = len(CHUNKS)
    for step in range(count + len(stages)):
        if step < count:
            grads(step)
            core_start(step)
        for j in range(count):
            if 0 <= step - j - 1 < len(stages):
                stages[step - j - 1](j)

    for copy in sent:
        copy.wait_send()

    @pl.when(is_enc)
    def _():
        drain(e_slope1)
        drain(e_slope0)
        drain(e_lg)

    drain(e_clip)
    drain(e_part)
    drain(e_lat1)
    drain(e_lat0)
    pltpu.make_async_copy(lg.at[pl.ds(0, 2)], latp, osem.at[0]).wait()
    for j in range(count):
        for copy in written(j):
            copy.wait()


def solution(mesh):
    T, S = mesh.shape["tm"], mesh.shape["space"]
    n = T * S
    shards = tuple(-(-len(blocks) * BLOCK // n // 16) * 16 for blocks in CHUNKS)
    sh = sum(shards)
    Y = S // 2
    half = n // 2 * sh
    count = len(CHUNKS)

    def on_device(clip_frames, enc_weight, dec_weight, out_grad):
        scale = 1.0 / math.sqrt(2 * 4 * 64 * n)
        dma = pltpu.SemaphoreType.DMA
        latp, wout = pl.pallas_call(
            functools.partial(kernel, T, S, shards, scale),
            out_shape=(
                jax.ShapeDtypeStruct((2, 4, 64, 256), BF),
                jax.ShapeDtypeStruct((9 * BLOCK, 128), BF),
            ),
            in_specs=[pl.BlockSpec(memory_space=pltpu.HBM)] * 4,
            out_specs=(pl.BlockSpec(memory_space=pl.ANY),) * 2,
            scratch_shapes=[
                pltpu.VMEM((4, 9, 128, 128), BF),
                pltpu.VMEM((4, 9, 64, 384), BF),
                pltpu.VMEM((9, 384, 256), BF),
                pltpu.VMEM((27, 256, 128), BF),
                pltpu.VMEM((9, 384, 256), BF),
                pltpu.VMEM((2, 4, 64, 128), BF),
                pltpu.VMEM((256, 256), BF),
                pltpu.VMEM((256, 256), BF),
                pltpu.VMEM((4, 6, 64, 256), BF),
                pltpu.VMEM((4, 6, 64, 128), BF),
                pltpu.VMEM((4, 6, 64, 384), BF),
                pltpu.VMEM((3, 4, 64, 256), BF),
                pltpu.VMEM((256, 768), BF),
                pltpu.VMEM((384, 512), BF),
                pltpu.VMEM((3, 256, 128), F32),
                pltpu.VMEM((n * sh, 128), BF),
                pltpu.VMEM((half, 128), BF),
                pltpu.VMEM((half, 128), BF),
                pltpu.VMEM((Y - 1, T * sh, 128), BF),
                pltpu.VMEM((T * sh, 128), BF),
                pltpu.VMEM((T - 1, sh, 128), BF),
                pltpu.VMEM((n * sh, 128), BF),
                dma((5,)),
                dma((24,)),
                dma((24,)),
                dma((2, count)),
                dma((2, count * (Y - 1))),
                dma((2, count * (T - 1))),
                dma((2, count * (T - 1))),
                dma((2, count * (Y - 1))),
                dma((2, count * Y)),
                dma((10,)),
            ],
            compiler_params=pltpu.CompilerParams(
                collective_id=0, has_side_effects=True, vmem_limit_bytes=60 * 1024 * 1024
            ),
            cost_estimate=pl.CostEstimate(
                flops=5 * 10**9, bytes_accessed=12 * 10**6, transcendentals=65536
            ),
        )(
            clip_frames,
            enc_weight.reshape(9, 384, 256),
            dec_weight.reshape(27, 256, 128),
            out_grad,
        )
        wide = pl.pallas_call(
            widen,
            grid=(6,),
            out_shape=jax.ShapeDtypeStruct((9 * BLOCK, 128), F32),
            in_specs=[pl.BlockSpec((9 * BLOCK // 6, 128), lambda i: (i, 0))],
            out_specs=pl.BlockSpec((9 * BLOCK // 6, 128), lambda i: (i, 0)),
            cost_estimate=pl.CostEstimate(flops=0, bytes_accessed=54 * BLOCK * 128, transcendentals=0),
        )(wout)
        return latp[None], wide.reshape(1, TAPS, 32768)

    placed = (P("tm", "space", None, None), P(), P(), P("tm", "space", None, None))
    return jax.shard_map(
        on_device,
        mesh=mesh,
        in_specs=placed,
        out_specs=(P("segment", "tm", "space", None, None), P("segment", None, None)),
        check_vma=False,
    )
```

```python
import functools
import math

import jax
import jax.numpy as jnp
from jax import lax
from jax.experimental import pallas as pl
from jax.experimental.pallas import tpu as pltpu
from jax.sharding import PartitionSpec as P

MESH = pl.DeviceIdType.MESH
BF = jnp.bfloat16
F32 = jnp.float32
TAPS = 27
BLOCK = 3 * 256
CHUNKS = (
    ((2, 0), (2, 1), (2, 2)),
    ((0, 0), (0, 1), (0, 2)),
    ((1, 0), (1, 1), (1, 2)),
)


def mm(x, y):
    return jnp.dot(x, y, preferred_element_type=F32)


def kernel(
    T,
    S,
    shards,
    scale,
    clip,
    ew_h,
    dw_h,
    og_h,
    latp,
    wout,
    clipx,
    x3,
    ew,
    dw,
    dwt,
    og,
    pout,
    pin,
    ext,
    rim,
    s3,
    lg,
    gt,
    st,
    mix,
    part,
    rcv1,
    red1,
    rcvy,
    red2,
    rcvz,
    gat,
    lsem,
    ssem,
    rsem,
    c_sem,
    y_sem,
    z_sem,
    gz_sem,
    gy_sem,
    gc_sem,
    gl_sem,
    osem,
):
    seg = lax.axis_index("segment")
    k = lax.axis_index("tm")
    s = lax.axis_index("space")
    n = T * S
    Y = S // 2
    core = s % 2
    y = s // 2
    has_up, has_dn = s > 0, s < S - 1
    has_pv, has_nx = k > 0, k < T - 1
    is_enc = seg == 0

    loads = [
        pltpu.make_async_copy(clip.at[pl.ds(2, 2)], clipx.at[pl.ds(2, 2), pl.ds(1, 8)], lsem.at[0]),
        pltpu.make_async_copy(ew_h, ew, lsem.at[1]),
        pltpu.make_async_copy(dw_h, dw, lsem.at[2]),
        pltpu.make_async_copy(og_h, og, lsem.at[3]),
        pltpu.make_async_copy(clip.at[pl.ds(0, 2)], clipx.at[pl.ds(0, 2), pl.ds(1, 8)], lsem.at[4]),
    ]
    for i in (0, 1, 4, 2, 3):
        loads[i].start()

    me = k * S + s
    barrier = pltpu.get_barrier_semaphore()

    def greet(d, carry):
        peer = (me + d) % n
        pl.semaphore_signal(
            barrier, inc=1, device_id=(seg, peer // S, peer % S), device_id_type=MESH
        )
        return carry

    lax.fori_loop(1, n, greet, 0)
    pl.semaphore_wait(barrier, n - 1)

    def remote(src, dst, i, to):
        return pltpu.make_async_remote_copy(
            src_ref=src,
            dst_ref=dst,
            send_sem=ssem.at[i],
            recv_sem=rsem.at[i],
            device_id=to,
            device_id_type=MESH,
        )

    def launch(entries):
        for copy, sends, gets, dst in entries:

            @pl.when(sends)
            def _():
                copy.start()

    def collect(entries):
        for copy, sends, gets, dst in entries:

            @pl.when(gets)
            def _():
                copy.wait_recv()

            @pl.when(jnp.logical_not(gets))
            def _():
                dst[...] = jnp.zeros(dst.shape, dst.dtype)

    def drain(entries):
        for copy, sends, gets, dst in entries:

            @pl.when(sends)
            def _():
                copy.wait_send()

    def entry(src, there, i, to, sends, gets):
        return (remote(src, there, i, to), sends, gets, there)

    def clip_entry(f, i):
        src = clip.at[pl.ds(f, 2), pl.ds(7, 1)]
        return entry(src, clipx.at[pl.ds(f, 2), pl.ds(0, 1)], i, (seg, k, s + 1), has_dn, has_up)

    e_clip = [clip_entry(2, 0), clip_entry(0, 23)]
    launch(e_clip)

    sel_i = lax.broadcasted_iota(jnp.int32, (192, 128), 0)
    sel_j = lax.broadcasted_iota(jnp.int32, (192, 128), 1)
    sel = (sel_j == 2 * (sel_i % 64) + sel_i // 64 - 1).astype(F32).astype(BF)

    def split_cols(f, r):
        y = mm(sel, clipx[f, r]).astype(BF)
        x3[f, r] = jnp.concatenate([y[:64], y[64:128], y[128:]], axis=1)

    def split_frame(f, carry):
        for r in range(1, 9):
            split_cols(f, r)
        return carry

    loads[0].wait()
    lax.fori_loop(2, 4, split_frame, 0)
    loads[1].wait()

    def xrows(f, b):
        return jnp.concatenate([x3[f, b + 2 * h] for h in range(4)], axis=0)

    acc = jnp.zeros((256, 256), F32)
    for a in range(2):
        for b in (1, 2):
            acc = acc + mm(xrows(2 + a, b), ew[3 * a + b])
    collect(e_clip[:1])
    for f in range(2, 4):
        split_cols(f, 0)
    for a in range(2):
        acc = acc + mm(xrows(2 + a, 0), ew[3 * a])
    pout[...] = acc.astype(BF)
    e_part = [entry(pout, pin, 1, (seg, k + 1, s), has_nx, has_pv)]
    launch(e_part)
    loads[4].wait()
    lax.fori_loop(0, 2, split_frame, 0)
    collect(e_clip[1:])
    for f in range(2):
        split_cols(f, 0)

    def lat_entries(f, base):
        own = 2 + f
        return [
            entry(ext.at[own, pl.ds(1, 4)], ext.at[f, pl.ds(1, 4)], base, (seg, k + 1, s), has_nx, has_pv),
            entry(ext.at[own, pl.ds(4, 1)], ext.at[own, pl.ds(0, 1)], base + 1, (seg, k, s + 1), has_dn, has_up),
            entry(ext.at[own, pl.ds(1, 1)], ext.at[own, pl.ds(5, 1)], base + 2, (seg, k, s - 1), has_up, has_dn),
            entry(
                ext.at[own, pl.ds(4, 1)],
                ext.at[f, pl.ds(0, 1)],
                base + 3,
                (seg, k + 1, s + 1),
                has_nx & has_dn,
                has_pv & has_up,
            ),
            entry(
                ext.at[own, pl.ds(1, 1)],
                ext.at[f, pl.ds(5, 1)],
                base + 4,
                (seg, k + 1, s - 1),
                has_nx & has_up,
                has_pv & has_dn,
            ),
        ]

    acc = jnp.zeros((256, 256), F32)
    for a in range(3):
        for b in range(3):
            acc = acc + mm(xrows(a, b), ew[3 * a + b])
    ext[3, 1:5] = acc.astype(BF).reshape(4, 64, 256)
    e_lat1 = lat_entries(1, 2)
    launch(e_lat1)

    acc = jnp.zeros((256, 256), F32)
    for b in range(3):
        acc = acc + mm(xrows(0, b), ew[6 + b])
    loads[2].wait()
    loads[3].wait()

    def turn(ab, carry):
        for c in range(3):
            dwt[ab, c * 128 : (c + 1) * 128, :] = dw[3 * ab + c].astype(F32).T.astype(BF)
        return carry

    @pl.when(is_enc)
    def _():
        lax.fori_loop(0, 4, turn, 0)

    collect(e_part)
    ext[2, 1:5] = (acc + pin[...].astype(F32)).astype(BF).reshape(4, 64, 256)
    e_lat0 = lat_entries(0, 7)
    launch(e_lat0)

    @pl.when(is_enc)
    def _():
        lax.fori_loop(4, 9, turn, 0)

    col = lax.broadcasted_iota(jnp.int32, (256, 128), 0) % 64

    def dcat(ab):
        return jnp.concatenate([dw[3 * ab], dw[3 * ab + 1], dw[3 * ab + 2]], axis=1)

    def erows(f, b):
        return jnp.concatenate([ext[f, b + h] for h in range(4)], axis=0)

    def decode(acc, t, taps_t):
        for a in taps_t:
            for b in range(3):
                acc = acc + mm(erows(t + a, b), dcat(3 * a + b))
        return acc

    def slope_of(acc, t):
        before = jnp.where(col == 0, 0.0, pltpu.roll(acc[:, :128], 1, 0))
        after = jnp.where(col == 63, 0.0, pltpu.roll(acc[:, 256:], 255, 0))
        pre = before + acc[:, 128:256] + after
        sg = jax.nn.sigmoid(pre)
        slope = og[t].reshape(256, 128).astype(F32) * sg * (1.0 + pre * (1.0 - sg))
        rim[t, 1:5] = slope.astype(BF).reshape(4, 64, 128)

    def slope_entries(f, base):
        own = rim.at[f, pl.ds(1, 4)]
        top = rim.at[f, pl.ds(1, 1)]
        last = rim.at[f, pl.ds(4, 1)]
        far = 2 + f
        return [
            entry(own, rim.at[far, pl.ds(1, 4)], base, (seg, k - 1, s), has_pv, has_nx),
            entry(last, rim.at[f, pl.ds(0, 1)], base + 1, (seg, k, s + 1), has_dn, has_up),
            entry(top, rim.at[f, pl.ds(5, 1)], base + 2, (seg, k, s - 1), has_up, has_dn),
            entry(last, rim.at[far, pl.ds(0, 1)], base + 3, (seg, k - 1, s + 1), has_pv & has_dn, has_nx & has_up),
            entry(top, rim.at[far, pl.ds(5, 1)], base + 4, (seg, k - 1, s - 1), has_pv & has_up, has_nx & has_dn),
        ]

    e_slope1 = slope_entries(1, 12)
    e_slope0 = slope_entries(0, 17)
    e_lg = [entry(lg.at[0], lg.at[2], 22, (seg, k - 1, s), has_pv, has_nx)]

    collect(e_lat1[1:3])
    collect(e_lat0[1:3])
    zero = jnp.zeros((256, 384), F32)
    acc1 = decode(zero, 1, (1, 2))
    acc0 = decode(zero, 0, (2,))
    collect(e_lat1[:1] + e_lat1[3:])
    slope_of(decode(acc1, 1, (0,)), 1)

    @pl.when(is_enc)
    def _():
        launch(e_slope1)

    acc0 = decode(acc0, 0, (1,))
    collect(e_lat0[:1] + e_lat0[3:])
    slope_of(decode(acc0, 0, (0,)), 0)

    @pl.when(is_enc)
    def _():
        launch(e_slope0)

    col64 = lax.broadcasted_iota(jnp.int32, (64, 128), 0)

    def shifts(v):
        later = jnp.where(col64 == 63, 0.0, pltpu.roll(v, 63, 0))
        sooner = jnp.where(col64 == 0, 0.0, pltpu.roll(v, 1, 0))
        return jnp.concatenate([later, v, sooner], axis=1)

    def put_shifts(f, which):
        for r in which:
            s3[f, r] = shifts(rim[f, r].astype(F32)).astype(BF)

    def transpose(acc, t, taps_t):
        for a in taps_t:
            for b in range(3):
                cells = jnp.concatenate([s3[t + 2 - a, h + 2 - b] for h in range(4)], axis=0)
                acc = acc + mm(cells, dwt[3 * a + b])
        return acc

    def keep(acc, t):
        rounded = acc.astype(BF)
        lg[t] = rounded.reshape(4, 64, 256)
        if t == 0:
            launch(e_lg)
        gt[:, t * 256 : (t + 1) * 256] = rounded.astype(F32).T.astype(BF)

    @pl.when(is_enc)
    def _():
        for f in (1, 0):
            put_shifts(f, range(1, 5))
        collect(e_slope1[1:3])
        collect(e_slope0[1:3])
        for f in (1, 0):
            put_shifts(f, (0, 5))
        zero = jnp.zeros((256, 256), F32)
        acc0 = transpose(zero, 0, (1, 2))
        acc1 = transpose(zero, 1, (2,))
        collect(e_slope1[:1] + e_slope1[3:])
        put_shifts(3, range(6))
        collect(e_slope0[:1] + e_slope0[3:])
        put_shifts(2, range(6))
        keep(transpose(acc0, 0, (0,)), 0)
        keep(transpose(acc1, 1, (0, 1)), 1)
        pltpu.make_async_copy(lg.at[pl.ds(0, 2)], latp, osem.at[0]).start()

    @pl.when(jnp.logical_not(is_enc))
    def _():
        pltpu.make_async_copy(ext.at[pl.ds(2, 2), pl.ds(1, 4)], latp, osem.at[0]).start()
        for t in range(2):
            cells = jnp.concatenate([shifts(rim[t, 1 + h].astype(F32)) for h in range(4)], axis=0)
            st[:, t * 256 : (t + 1) * 256] = cells.T.astype(BF)

    def enc_block(a, b, at):
        frames, lanes = (1, 3) if a == 1 else (0, 2), 0 if a == 2 else 256
        cells = jnp.concatenate([xrows(f, b) for f in frames], axis=0)
        grad = mm(gt[:, lanes : lanes + 512], cells)
        for c in range(3):
            whole = grad[:, c * 128 : (c + 1) * 128].T
            mix[c, pl.ds(0, 128, stride=2), :] = whole[:, :128]
            mix[c, pl.ds(1, 128, stride=2), :] = whole[:, 128:]
            part[at + c * 256 : at + (c + 1) * 256, :] = mix[c].astype(BF)

    def dec_block(a, b, at):
        cells = jnp.concatenate([erows(a, b), erows(1 + a, b)], axis=0)
        grad = mm(st[...], cells)
        for c in range(3):
            part[at + c * 256 : at + (c + 1) * 256, :] = grad[c * 128 : (c + 1) * 128].T.astype(BF)

    sh = shards
    off = [sum(sh[:j]) for j in range(len(sh))]

    def grads(j):
        at = off[j] * n

        @pl.when(is_enc)
        def _():
            if CHUNKS[j][0] == (0, 0):
                collect(e_lg)
                gt[:, 512:768] = lg[2].reshape(256, 256).astype(F32).T.astype(BF)
            for i, (a, b) in enumerate(CHUNKS[j]):
                enc_block(a, b, at + i * BLOCK)

        @pl.when(jnp.logical_not(is_enc))
        def _():
            for i, (a, b) in enumerate(CHUNKS[j]):
                dec_block(a, b, at + i * BLOCK)

        used = BLOCK * len(CHUNKS[j])
        if n * sh[j] > used:
            part[at + used : at + n * sh[j], :] = jnp.zeros((n * sh[j] - used, 128), BF)

    def rows(start, count):
        return pl.ds(pl.multiple_of(start, 16), count)

    def move(src, dst, sems, i, to):
        return pltpu.make_async_remote_copy(
            src_ref=src,
            dst_ref=dst,
            send_sem=sems.at[0, i],
            recv_sem=sems.at[1, i],
            device_id=to,
            device_id_type=MESH,
        )

    sibling = (seg, k, s + 1 - 2 * core)
    sent = []

    def send(copy):
        copy.start()
        sent.append(copy)

    def arrived(dst, sems, i):
        move(dst, dst, sems, i, sibling).wait_recv()

    def at_y(p):
        return (seg, k, 2 * p + core)

    last = len(CHUNKS) - 1

    def half_of(ref, j):
        return ref.at[off[j] * n // 2 : off[j] * n // 2 + sh[j] * n // 2]

    def core_start(j):
        away = part.at[rows(off[j] * n + (1 - core) * (sh[j] * n // 2), sh[j] * n // 2)]
        send(move(away, half_of(rcv1, j), c_sem, j, sibling))

    def y_start(j):
        count = sh[j] * n // 2
        lo = off[j] * n // 2
        arrived(half_of(rcv1, j), c_sem, j)
        own = part[rows(off[j] * n + core * count, count), :].astype(F32)
        red1[lo : lo + count, :] = (own + rcv1[lo : lo + count, :].astype(F32)).astype(BF)
        for d in range(1, Y):
            p = (y + d) % Y
            i = j * (Y - 1) + d - 1
            slot = rcvy.at[d - 1, off[j] * T : (off[j] + sh[j]) * T]
            send(move(red1.at[rows(lo + p * T * sh[j], T * sh[j])], slot, y_sem, i, at_y(p)))

    def z_start(j):
        lo, count = off[j] * T, sh[j] * T
        total = red1[rows(off[j] * n // 2 + y * count, count), :].astype(F32)
        for d in range(1, Y):
            arrived(rcvy.at[d - 1, lo : lo + count], y_sem, j * (Y - 1) + d - 1)
            total = total + rcvy[d - 1, lo : lo + count, :].astype(F32)
        red2[lo : lo + count, :] = total.astype(BF)
        for d in range(1, T):
            p = (k + d) % T
            i = j * (T - 1) + d - 1
            slot = rcvz.at[d - 1, off[j] : off[j] + sh[j]]
            send(move(red2.at[rows(lo + p * sh[j], sh[j])], slot, z_sem, i, (seg, p, s)))

    def shard(j, py, pz):
        return rows(off[j] * n + ((core * Y + py) * T + pz) * sh[j], sh[j])

    def band(j, pc, py):
        return gat.at[rows(off[j] * n + (pc * Y + py) * T * sh[j], T * sh[j])]

    def gz_start(j):
        total = red2[rows(off[j] * T + k * sh[j], sh[j]), :].astype(F32)
        for d in range(1, T):
            arrived(rcvz.at[d - 1, off[j] : off[j] + sh[j]], z_sem, j * (T - 1) + d - 1)
            total = total + rcvz[d - 1, off[j] : off[j] + sh[j], :].astype(F32)
        mine = shard(j, y, k)
        gat[mine, :] = (total * scale).astype(BF)
        for d in range(1, T):
            send(move(gat.at[mine], gat.at[mine], gz_sem, j * (T - 1) + d - 1, (seg, (k + d) % T, s)))
        if j == last:
            for d in range(1, Y):
                for e in range(T):
                    to = (seg, (k + e) % T, 2 * ((y + d) % Y) + core)
                    send(move(gat.at[mine], gat.at[mine], gl_sem, (d - 1) * T + e, to))

    def gy_start(j):
        for d in range(1, T):
            arrived(gat.at[shard(j, y, (k - d + T) % T)], gz_sem, j * (T - 1) + d - 1)
        mine = band(j, core, y)
        for d in range(1, Y if j != last else 1):
            send(move(mine, mine, gy_sem, j * (Y - 1) + d - 1, at_y((y + d) % Y)))
        send(move(mine, mine, gc_sem, j * Y, sibling))

    def gc_start(j):
        for d in range(1, Y):
            theirs = band(j, core, (y - d + Y) % Y)
            if j == last:
                for e in range(T):
                    piece = gat.at[shard(j, (y - d + Y) % Y, (k - e + T) % T)]
                    arrived(piece, gl_sem, (d - 1) * T + e)
            else:
                arrived(theirs, gy_sem, j * (Y - 1) + d - 1)
            send(move(theirs, theirs, gc_sem, j * Y + d, sibling))

    def written(j):
        copies = []
        for i, (a, b) in enumerate(CHUNKS[j]):
            src = gat.at[off[j] * n + i * BLOCK : off[j] * n + (i + 1) * BLOCK]
            dst = wout.at[(3 * a + b) * BLOCK : (3 * a + b + 1) * BLOCK]
            copies.append(pltpu.make_async_copy(src, dst, osem.at[1 + 3 * a + b]))
        return copies

    def finish(j):
        for d in range(Y):
            arrived(band(j, 1 - core, (y - d + Y) % Y), gc_sem, j * Y + d)
        for copy in written(j):
            copy.start()

    stages = [y_start, z_start, gz_start, gy_start, gc_start, finish]
    count = len(CHUNKS)
    for step in range(count + len(stages)):
        if step < count:
            grads(step)
            core_start(step)
        for j in range(count):
            if 0 <= step - j - 1 < len(stages):
                stages[step - j - 1](j)

    for copy in sent:
        copy.wait_send()

    @pl.when(is_enc)
    def _():
        drain(e_slope1)
        drain(e_slope0)
        drain(e_lg)

    drain(e_clip)
    drain(e_part)
    drain(e_lat1)
    drain(e_lat0)
    pltpu.make_async_copy(lg.at[pl.ds(0, 2)], latp, osem.at[0]).wait()
    for j in range(count):
        for copy in written(j):
            copy.wait()


def solution(mesh):
    T, S = mesh.shape["tm"], mesh.shape["space"]
    n = T * S
    shards = tuple(-(-len(blocks) * BLOCK // n // 16) * 16 for blocks in CHUNKS)
    sh = sum(shards)
    Y = S // 2
    half = n // 2 * sh
    count = len(CHUNKS)

    def on_device(clip_frames, enc_weight, dec_weight, out_grad):
        scale = 1.0 / math.sqrt(2 * 4 * 64 * n)
        dma = pltpu.SemaphoreType.DMA
        latp, wout = pl.pallas_call(
            functools.partial(kernel, T, S, shards, scale),
            out_shape=(
                jax.ShapeDtypeStruct((2, 4, 64, 256), BF),
                jax.ShapeDtypeStruct((9 * BLOCK, 128), BF),
            ),
            in_specs=[pl.BlockSpec(memory_space=pltpu.HBM)] * 4,
            out_specs=(pl.BlockSpec(memory_space=pl.ANY),) * 2,
            scratch_shapes=[
                pltpu.VMEM((4, 9, 128, 128), BF),
                pltpu.VMEM((4, 9, 64, 384), BF),
                pltpu.VMEM((9, 384, 256), BF),
                pltpu.VMEM((27, 256, 128), BF),
                pltpu.VMEM((9, 384, 256), BF),
                pltpu.VMEM((2, 4, 64, 128), BF),
                pltpu.VMEM((256, 256), BF),
                pltpu.VMEM((256, 256), BF),
                pltpu.VMEM((4, 6, 64, 256), BF),
                pltpu.VMEM((4, 6, 64, 128), BF),
                pltpu.VMEM((4, 6, 64, 384), BF),
                pltpu.VMEM((3, 4, 64, 256), BF),
                pltpu.VMEM((256, 768), BF),
                pltpu.VMEM((384, 512), BF),
                pltpu.VMEM((3, 256, 128), F32),
                pltpu.VMEM((n * sh, 128), BF),
                pltpu.VMEM((half, 128), BF),
                pltpu.VMEM((half, 128), BF),
                pltpu.VMEM((Y - 1, T * sh, 128), BF),
                pltpu.VMEM((T * sh, 128), BF),
                pltpu.VMEM((T - 1, sh, 128), BF),
                pltpu.VMEM((n * sh, 128), BF),
                dma((5,)),
                dma((24,)),
                dma((24,)),
                dma((2, count)),
                dma((2, count * (Y - 1))),
                dma((2, count * (T - 1))),
                dma((2, count * (T - 1))),
                dma((2, count * (Y - 1))),
                dma((2, count * Y)),
                dma((2, (Y - 1) * T)),
                dma((10,)),
            ],
            compiler_params=pltpu.CompilerParams(
                collective_id=0, has_side_effects=True, vmem_limit_bytes=60 * 1024 * 1024
            ),
            cost_estimate=pl.CostEstimate(
                flops=5 * 10**9, bytes_accessed=12 * 10**6, transcendentals=65536
            ),
        )(
            clip_frames,
            enc_weight.reshape(9, 384, 256),
            dec_weight.reshape(27, 256, 128),
            out_grad,
        )
        return latp[None], wout.reshape(1, TAPS, 32768).astype(F32)

    placed = (P("tm", "space", None, None), P(), P(), P("tm", "space", None, None))
    return jax.shard_map(
        on_device,
        mesh=mesh,
        in_specs=placed,
        out_specs=(P("segment", "tm", "space", None, None), P("segment", None, None)),
        check_vma=False,
    )
```

```python
import functools
import math

import jax
import jax.numpy as jnp
from jax import lax
from jax.experimental import pallas as pl
from jax.experimental.pallas import tpu as pltpu
from jax.sharding import PartitionSpec as P

MESH = pl.DeviceIdType.MESH
BF = jnp.bfloat16
F32 = jnp.float32
TAPS = 27
BLOCK = 3 * 256
CHUNKS = (
    ((2, 0), (2, 1), (2, 2)),
    ((0, 0), (0, 1), (0, 2)),
    ((1, 0), (1, 1), (1, 2)),
)


def mm(x, y):
    return jnp.dot(x, y, preferred_element_type=F32)


def kernel(
    T,
    S,
    shards,
    clip,
    ew_h,
    dw_h,
    og_h,
    latp,
    wout,
    clipx,
    x3,
    ew,
    dw,
    dwt,
    og,
    pout,
    pin,
    ext,
    rim,
    s3,
    lg,
    gt,
    st,
    mix,
    part,
    rcv1,
    red1,
    rcvy,
    red2,
    rcvz,
    gat,
    wide,
    lsem,
    ssem,
    rsem,
    c_sem,
    y_sem,
    z_sem,
    gz_sem,
    gy_sem,
    gc_sem,
    gl_sem,
    osem,
):
    seg = lax.axis_index("segment")
    k = lax.axis_index("tm")
    s = lax.axis_index("space")
    n = T * S
    Y = S // 2
    core = s % 2
    y = s // 2
    has_up, has_dn = s > 0, s < S - 1
    has_pv, has_nx = k > 0, k < T - 1
    is_enc = seg == 0

    loads = [
        pltpu.make_async_copy(clip.at[pl.ds(2, 2)], clipx.at[pl.ds(2, 2), pl.ds(1, 8)], lsem.at[0]),
        pltpu.make_async_copy(ew_h, ew, lsem.at[1]),
        pltpu.make_async_copy(dw_h, dw, lsem.at[2]),
        pltpu.make_async_copy(og_h, og, lsem.at[3]),
        pltpu.make_async_copy(clip.at[pl.ds(0, 2)], clipx.at[pl.ds(0, 2), pl.ds(1, 8)], lsem.at[4]),
    ]
    for i in (0, 1, 4, 2, 3):
        loads[i].start()

    me = k * S + s
    barrier = pltpu.get_barrier_semaphore()

    def greet(d, carry):
        peer = (me + d) % n
        pl.semaphore_signal(
            barrier, inc=1, device_id=(seg, peer // S, peer % S), device_id_type=MESH
        )
        return carry

    lax.fori_loop(1, n, greet, 0)
    pl.semaphore_wait(barrier, n - 1)

    def remote(src, dst, i, to):
        return pltpu.make_async_remote_copy(
            src_ref=src,
            dst_ref=dst,
            send_sem=ssem.at[i],
            recv_sem=rsem.at[i],
            device_id=to,
            device_id_type=MESH,
        )

    def launch(entries):
        for copy, sends, gets, dst in entries:

            @pl.when(sends)
            def _():
                copy.start()

    def collect(entries):
        for copy, sends, gets, dst in entries:

            @pl.when(gets)
            def _():
                copy.wait_recv()

            @pl.when(jnp.logical_not(gets))
            def _():
                dst[...] = jnp.zeros(dst.shape, dst.dtype)

    def drain(entries):
        for copy, sends, gets, dst in entries:

            @pl.when(sends)
            def _():
                copy.wait_send()

    def entry(src, there, i, to, sends, gets):
        return (remote(src, there, i, to), sends, gets, there)

    def clip_entry(f, i):
        src = clip.at[pl.ds(f, 2), pl.ds(7, 1)]
        return entry(src, clipx.at[pl.ds(f, 2), pl.ds(0, 1)], i, (seg, k, s + 1), has_dn, has_up)

    e_clip = [clip_entry(2, 0), clip_entry(0, 23)]
    launch(e_clip)

    sel_i = lax.broadcasted_iota(jnp.int32, (192, 128), 0)
    sel_j = lax.broadcasted_iota(jnp.int32, (192, 128), 1)
    sel = (sel_j == 2 * (sel_i % 64) + sel_i // 64 - 1).astype(F32).astype(BF)

    def split_cols(f, r):
        y = mm(sel, clipx[f, r]).astype(BF)
        x3[f, r] = jnp.concatenate([y[:64], y[64:128], y[128:]], axis=1)

    def split_frame(f, carry):
        for r in range(1, 9):
            split_cols(f, r)
        return carry

    loads[0].wait()
    lax.fori_loop(2, 4, split_frame, 0)
    loads[1].wait()

    def xrows(f, b):
        return jnp.concatenate([x3[f, b + 2 * h] for h in range(4)], axis=0)

    acc = jnp.zeros((256, 256), F32)
    for a in range(2):
        for b in (1, 2):
            acc = acc + mm(xrows(2 + a, b), ew[3 * a + b])
    collect(e_clip[:1])
    for f in range(2, 4):
        split_cols(f, 0)
    for a in range(2):
        acc = acc + mm(xrows(2 + a, 0), ew[3 * a])
    pout[...] = acc.astype(BF)
    e_part = [entry(pout, pin, 1, (seg, k + 1, s), has_nx, has_pv)]
    launch(e_part)
    loads[4].wait()
    lax.fori_loop(0, 2, split_frame, 0)
    collect(e_clip[1:])
    for f in range(2):
        split_cols(f, 0)

    def lat_entries(f, base):
        own = 2 + f
        return [
            entry(ext.at[own, pl.ds(1, 4)], ext.at[f, pl.ds(1, 4)], base, (seg, k + 1, s), has_nx, has_pv),
            entry(ext.at[own, pl.ds(4, 1)], ext.at[own, pl.ds(0, 1)], base + 1, (seg, k, s + 1), has_dn, has_up),
            entry(ext.at[own, pl.ds(1, 1)], ext.at[own, pl.ds(5, 1)], base + 2, (seg, k, s - 1), has_up, has_dn),
            entry(
                ext.at[own, pl.ds(4, 1)],
                ext.at[f, pl.ds(0, 1)],
                base + 3,
                (seg, k + 1, s + 1),
                has_nx & has_dn,
                has_pv & has_up,
            ),
            entry(
                ext.at[own, pl.ds(1, 1)],
                ext.at[f, pl.ds(5, 1)],
                base + 4,
                (seg, k + 1, s - 1),
                has_nx & has_up,
                has_pv & has_dn,
            ),
        ]

    acc = jnp.zeros((256, 256), F32)
    for a in range(3):
        for b in range(3):
            acc = acc + mm(xrows(a, b), ew[3 * a + b])
    ext[3, 1:5] = acc.astype(BF).reshape(4, 64, 256)
    e_lat1 = lat_entries(1, 2)
    launch(e_lat1)

    acc = jnp.zeros((256, 256), F32)
    for b in range(3):
        acc = acc + mm(xrows(0, b), ew[6 + b])
    loads[2].wait()
    loads[3].wait()

    def turn(ab, carry):
        for c in range(3):
            dwt[ab, c * 128 : (c + 1) * 128, :] = dw[3 * ab + c].astype(F32).T.astype(BF)
        return carry

    @pl.when(is_enc)
    def _():
        lax.fori_loop(0, 4, turn, 0)

    collect(e_part)
    ext[2, 1:5] = (acc + pin[...].astype(F32)).astype(BF).reshape(4, 64, 256)
    e_lat0 = lat_entries(0, 7)
    launch(e_lat0)

    @pl.when(is_enc)
    def _():
        lax.fori_loop(4, 9, turn, 0)

    col = lax.broadcasted_iota(jnp.int32, (256, 128), 0) % 64

    def dcat(ab):
        return jnp.concatenate([dw[3 * ab], dw[3 * ab + 1], dw[3 * ab + 2]], axis=1)

    def erows(f, b):
        return jnp.concatenate([ext[f, b + h] for h in range(4)], axis=0)

    def decode(acc, t, taps_t):
        for a in taps_t:
            for b in range(3):
                acc = acc + mm(erows(t + a, b), dcat(3 * a + b))
        return acc

    def slope_of(acc, t):
        before = jnp.where(col == 0, 0.0, pltpu.roll(acc[:, :128], 1, 0))
        after = jnp.where(col == 63, 0.0, pltpu.roll(acc[:, 256:], 255, 0))
        pre = before + acc[:, 128:256] + after
        sg = jax.nn.sigmoid(pre)
        slope = og[t].reshape(256, 128).astype(F32) * sg * (1.0 + pre * (1.0 - sg))
        rim[t, 1:5] = slope.astype(BF).reshape(4, 64, 128)

    def slope_entries(f, base):
        own = rim.at[f, pl.ds(1, 4)]
        top = rim.at[f, pl.ds(1, 1)]
        last = rim.at[f, pl.ds(4, 1)]
        far = 2 + f
        return [
            entry(own, rim.at[far, pl.ds(1, 4)], base, (seg, k - 1, s), has_pv, has_nx),
            entry(last, rim.at[f, pl.ds(0, 1)], base + 1, (seg, k, s + 1), has_dn, has_up),
            entry(top, rim.at[f, pl.ds(5, 1)], base + 2, (seg, k, s - 1), has_up, has_dn),
            entry(last, rim.at[far, pl.ds(0, 1)], base + 3, (seg, k - 1, s + 1), has_pv & has_dn, has_nx & has_up),
            entry(top, rim.at[far, pl.ds(5, 1)], base + 4, (seg, k - 1, s - 1), has_pv & has_up, has_nx & has_dn),
        ]

    e_slope1 = slope_entries(1, 12)
    e_slope0 = slope_entries(0, 17)
    e_lg = [entry(lg.at[0], lg.at[2], 22, (seg, k - 1, s), has_pv, has_nx)]

    collect(e_lat1[1:3])
    collect(e_lat0[1:3])
    zero = jnp.zeros((256, 384), F32)
    acc1 = decode(zero, 1, (1, 2))
    acc0 = decode(zero, 0, (2,))
    collect(e_lat1[:1] + e_lat1[3:])
    slope_of(decode(acc1, 1, (0,)), 1)

    @pl.when(is_enc)
    def _():
        launch(e_slope1)

    acc0 = decode(acc0, 0, (1,))
    collect(e_lat0[:1] + e_lat0[3:])
    slope_of(decode(acc0, 0, (0,)), 0)

    @pl.when(is_enc)
    def _():
        launch(e_slope0)

    col64 = lax.broadcasted_iota(jnp.int32, (64, 128), 0)

    def shifts(v):
        later = jnp.where(col64 == 63, 0.0, pltpu.roll(v, 63, 0))
        sooner = jnp.where(col64 == 0, 0.0, pltpu.roll(v, 1, 0))
        return jnp.concatenate([later, v, sooner], axis=1)

    def put_shifts(f, which):
        for r in which:
            s3[f, r] = shifts(rim[f, r].astype(F32)).astype(BF)

    def transpose(acc, t, taps_t):
        for a in taps_t:
            for b in range(3):
                cells = jnp.concatenate([s3[t + 2 - a, h + 2 - b] for h in range(4)], axis=0)
                acc = acc + mm(cells, dwt[3 * a + b])
        return acc

    def keep(acc, t):
        rounded = acc.astype(BF)
        lg[t] = rounded.reshape(4, 64, 256)
        if t == 0:
            launch(e_lg)
        gt[:, t * 256 : (t + 1) * 256] = rounded.astype(F32).T.astype(BF)

    @pl.when(is_enc)
    def _():
        for f in (1, 0):
            put_shifts(f, range(1, 5))
        collect(e_slope1[1:3])
        collect(e_slope0[1:3])
        for f in (1, 0):
            put_shifts(f, (0, 5))
        zero = jnp.zeros((256, 256), F32)
        acc0 = transpose(zero, 0, (1, 2))
        acc1 = transpose(zero, 1, (2,))
        collect(e_slope1[:1] + e_slope1[3:])
        put_shifts(3, range(6))
        collect(e_slope0[:1] + e_slope0[3:])
        put_shifts(2, range(6))
        keep(transpose(acc0, 0, (0,)), 0)
        keep(transpose(acc1, 1, (0, 1)), 1)
        pltpu.make_async_copy(lg.at[pl.ds(0, 2)], latp, osem.at[0]).start()

    @pl.when(jnp.logical_not(is_enc))
    def _():
        pltpu.make_async_copy(ext.at[pl.ds(2, 2), pl.ds(1, 4)], latp, osem.at[0]).start()
        for t in range(2):
            cells = jnp.concatenate([shifts(rim[t, 1 + h].astype(F32)) for h in range(4)], axis=0)
            st[:, t * 256 : (t + 1) * 256] = cells.T.astype(BF)

    def enc_block(a, b, at):
        frames, lanes = (1, 3) if a == 1 else (0, 2), 0 if a == 2 else 256
        cells = jnp.concatenate([xrows(f, b) for f in frames], axis=0)
        grad = mm(gt[:, lanes : lanes + 512], cells)
        for c in range(3):
            whole = grad[:, c * 128 : (c + 1) * 128].T
            mix[c, pl.ds(0, 128, stride=2), :] = whole[:, :128]
            mix[c, pl.ds(1, 128, stride=2), :] = whole[:, 128:]
            part[at + c * 256 : at + (c + 1) * 256, :] = mix[c].astype(BF)

    def dec_block(a, b, at):
        cells = jnp.concatenate([erows(a, b), erows(1 + a, b)], axis=0)
        grad = mm(st[...], cells)
        for c in range(3):
            part[at + c * 256 : at + (c + 1) * 256, :] = grad[c * 128 : (c + 1) * 128].T.astype(BF)

    sh = shards
    off = [sum(sh[:j]) for j in range(len(sh))]

    def grads(j):
        at = off[j] * n

        @pl.when(is_enc)
        def _():
            if CHUNKS[j][0] == (0, 0):
                collect(e_lg)
                gt[:, 512:768] = lg[2].reshape(256, 256).astype(F32).T.astype(BF)
            for i, (a, b) in enumerate(CHUNKS[j]):
                enc_block(a, b, at + i * BLOCK)

        @pl.when(jnp.logical_not(is_enc))
        def _():
            for i, (a, b) in enumerate(CHUNKS[j]):
                dec_block(a, b, at + i * BLOCK)

        used = BLOCK * len(CHUNKS[j])
        if n * sh[j] > used:
            part[at + used : at + n * sh[j], :] = jnp.zeros((n * sh[j] - used, 128), BF)

    def rows(start, count):
        return pl.ds(pl.multiple_of(start, 16), count)

    def move(src, dst, sems, i, to):
        return pltpu.make_async_remote_copy(
            src_ref=src,
            dst_ref=dst,
            send_sem=sems.at[0, i],
            recv_sem=sems.at[1, i],
            device_id=to,
            device_id_type=MESH,
        )

    sibling = (seg, k, s + 1 - 2 * core)
    sent = []

    def send(copy):
        copy.start()
        sent.append(copy)

    def arrived(dst, sems, i):
        move(dst, dst, sems, i, sibling).wait_recv()

    def at_y(p):
        return (seg, k, 2 * p + core)

    last = len(CHUNKS) - 1

    def half_of(ref, j):
        return ref.at[off[j] * n // 2 : off[j] * n // 2 + sh[j] * n // 2]

    def core_start(j):
        away = part.at[rows(off[j] * n + (1 - core) * (sh[j] * n // 2), sh[j] * n // 2)]
        send(move(away, half_of(rcv1, j), c_sem, j, sibling))

    def y_start(j):
        count = sh[j] * n // 2
        lo = off[j] * n // 2
        arrived(half_of(rcv1, j), c_sem, j)
        own = part[rows(off[j] * n + core * count, count), :].astype(F32)
        red1[lo : lo + count, :] = (own + rcv1[lo : lo + count, :].astype(F32)).astype(BF)
        for d in range(1, Y):
            p = (y + d) % Y
            i = j * (Y - 1) + d - 1
            slot = rcvy.at[d - 1, off[j] * T : (off[j] + sh[j]) * T]
            send(move(red1.at[rows(lo + p * T * sh[j], T * sh[j])], slot, y_sem, i, at_y(p)))

    def z_start(j):
        lo, count = off[j] * T, sh[j] * T
        total = red1[rows(off[j] * n // 2 + y * count, count), :].astype(F32)
        for d in range(1, Y):
            arrived(rcvy.at[d - 1, lo : lo + count], y_sem, j * (Y - 1) + d - 1)
            total = total + rcvy[d - 1, lo : lo + count, :].astype(F32)
        red2[lo : lo + count, :] = total.astype(BF)
        for d in range(1, T):
            p = (k + d) % T
            i = j * (T - 1) + d - 1
            slot = rcvz.at[d - 1, off[j] : off[j] + sh[j]]
            send(move(red2.at[rows(lo + p * sh[j], sh[j])], slot, z_sem, i, (seg, p, s)))

    def shard(j, py, pz):
        return rows(off[j] * n + ((core * Y + py) * T + pz) * sh[j], sh[j])

    def band(j, pc, py):
        return gat.at[rows(off[j] * n + (pc * Y + py) * T * sh[j], T * sh[j])]

    def gz_start(j):
        total = red2[rows(off[j] * T + k * sh[j], sh[j]), :].astype(F32)
        for d in range(1, T):
            arrived(rcvz.at[d - 1, off[j] : off[j] + sh[j]], z_sem, j * (T - 1) + d - 1)
            total = total + rcvz[d - 1, off[j] : off[j] + sh[j], :].astype(F32)
        mine = shard(j, y, k)
        gat[mine, :] = total.astype(BF)
        for d in range(1, T):
            send(move(gat.at[mine], gat.at[mine], gz_sem, j * (T - 1) + d - 1, (seg, (k + d) % T, s)))
        if j == last:
            for d in range(1, Y):
                for e in range(T):
                    to = (seg, (k + e) % T, 2 * ((y + d) % Y) + core)
                    send(move(gat.at[mine], gat.at[mine], gl_sem, (d - 1) * T + e, to))

    def gy_start(j):
        for d in range(1, T):
            arrived(gat.at[shard(j, y, (k - d + T) % T)], gz_sem, j * (T - 1) + d - 1)
        mine = band(j, core, y)
        for d in range(1, Y if j != last else 1):
            send(move(mine, mine, gy_sem, j * (Y - 1) + d - 1, at_y((y + d) % Y)))
        send(move(mine, mine, gc_sem, j * Y, sibling))

    def gc_start(j):
        for d in range(1, Y):
            theirs = band(j, core, (y - d + Y) % Y)
            if j == last:
                for e in range(T):
                    piece = gat.at[shard(j, (y - d + Y) % Y, (k - e + T) % T)]
                    arrived(piece, gl_sem, (d - 1) * T + e)
            else:
                arrived(theirs, gy_sem, j * (Y - 1) + d - 1)
            send(move(theirs, theirs, gc_sem, j * Y + d, sibling))

    def written(j):
        copies = []
        for i, (a, b) in enumerate(CHUNKS[j]):
            src = wide.at[off[j] * n + i * BLOCK : off[j] * n + (i + 1) * BLOCK]
            dst = wout.at[(3 * a + b) * BLOCK : (3 * a + b + 1) * BLOCK]
            copies.append(pltpu.make_async_copy(src, dst, osem.at[1 + 3 * a + b]))
        return copies

    def finish(j):
        for d in range(Y):
            arrived(band(j, 1 - core, (y - d + Y) % Y), gc_sem, j * Y + d)
        used = slice(off[j] * n, off[j] * n + len(CHUNKS[j]) * BLOCK)
        wide[used, :] = gat[used, :].astype(F32)
        for copy in written(j):
            copy.start()

    stages = [y_start, z_start, gz_start, gy_start, gc_start, finish]
    count = len(CHUNKS)
    for step in range(count + len(stages)):
        if step < count:
            grads(step)
            core_start(step)
        for j in range(count):
            if 0 <= step - j - 1 < len(stages):
                stages[step - j - 1](j)

    for copy in sent:
        copy.wait_send()

    @pl.when(is_enc)
    def _():
        drain(e_slope1)
        drain(e_slope0)
        drain(e_lg)

    drain(e_clip)
    drain(e_part)
    drain(e_lat1)
    drain(e_lat0)
    pltpu.make_async_copy(lg.at[pl.ds(0, 2)], latp, osem.at[0]).wait()
    for j in range(count):
        for copy in written(j):
            copy.wait()


def solution(mesh):
    T, S = mesh.shape["tm"], mesh.shape["space"]
    n = T * S
    shards = tuple(-(-len(blocks) * BLOCK // n // 16) * 16 for blocks in CHUNKS)
    sh = sum(shards)
    Y = S // 2
    half = n // 2 * sh
    count = len(CHUNKS)

    def on_device(clip_frames, enc_weight, dec_weight, out_grad):
        scale = 1.0 / math.sqrt(2 * 4 * 64 * n)
        dma = pltpu.SemaphoreType.DMA
        latp, wout = pl.pallas_call(
            functools.partial(kernel, T, S, shards),
            out_shape=(
                jax.ShapeDtypeStruct((2, 4, 64, 256), BF),
                jax.ShapeDtypeStruct((9 * BLOCK, 128), F32),
            ),
            in_specs=[pl.BlockSpec(memory_space=pltpu.HBM)] * 4,
            out_specs=(pl.BlockSpec(memory_space=pl.ANY),) * 2,
            scratch_shapes=[
                pltpu.VMEM((4, 9, 128, 128), BF),
                pltpu.VMEM((4, 9, 64, 384), BF),
                pltpu.VMEM((9, 384, 256), BF),
                pltpu.VMEM((27, 256, 128), BF),
                pltpu.VMEM((9, 384, 256), BF),
                pltpu.VMEM((2, 4, 64, 128), BF),
                pltpu.VMEM((256, 256), BF),
                pltpu.VMEM((256, 256), BF),
                pltpu.VMEM((4, 6, 64, 256), BF),
                pltpu.VMEM((4, 6, 64, 128), BF),
                pltpu.VMEM((4, 6, 64, 384), BF),
                pltpu.VMEM((3, 4, 64, 256), BF),
                pltpu.VMEM((256, 768), BF),
                pltpu.VMEM((384, 512), BF),
                pltpu.VMEM((3, 256, 128), F32),
                pltpu.VMEM((n * sh, 128), BF),
                pltpu.VMEM((half, 128), BF),
                pltpu.VMEM((half, 128), BF),
                pltpu.VMEM((Y - 1, T * sh, 128), BF),
                pltpu.VMEM((T * sh, 128), BF),
                pltpu.VMEM((T - 1, sh, 128), BF),
                pltpu.VMEM((n * sh, 128), BF),
                pltpu.VMEM((n * sh, 128), F32),
                dma((5,)),
                dma((24,)),
                dma((24,)),
                dma((2, count)),
                dma((2, count * (Y - 1))),
                dma((2, count * (T - 1))),
                dma((2, count * (T - 1))),
                dma((2, count * (Y - 1))),
                dma((2, count * Y)),
                dma((2, (Y - 1) * T)),
                dma((10,)),
            ],
            compiler_params=pltpu.CompilerParams(
                collective_id=0, has_side_effects=True, vmem_limit_bytes=60 * 1024 * 1024
            ),
            cost_estimate=pl.CostEstimate(
                flops=5 * 10**9, bytes_accessed=12 * 10**6, transcendentals=65536
            ),
        )(
            clip_frames,
            enc_weight.reshape(9, 384, 256),
            dec_weight.reshape(27, 256, 128),
            out_grad,
        )
        return latp[None], (wout * scale).reshape(1, TAPS, 32768)

    placed = (P("tm", "space", None, None), P(), P(), P("tm", "space", None, None))
    return jax.shard_map(
        on_device,
        mesh=mesh,
        in_specs=placed,
        out_specs=(P("segment", "tm", "space", None, None), P("segment", None, None)),
        check_vma=False,
    )
```
